256 devices in a mesh: vertex: 16 (over z, core), feat: 16 (over x, y).
Axes of the slice: x: 4, y: 4, z: 8, core: 2. Of those that a mesh axis runs over, the one named last changes fastest.
Arguments:
- features: bfloat16 [768, 65536], P('feat', 'vertex'), may hold values from -6 to 6
- neigh_weight: bfloat16 [768, 1024], P('feat'), may hold values from -0.3125 to 0.3125
- self_weight: bfloat16 [768, 1024], P('feat'), may hold values from -0.21875 to 0.21875
- bias: bfloat16 [1024], P('feat'), may hold values from -1 to 1
- neighbors: int32 [25, 32768], P(None, 'vertex'), may hold values from -1 to 8191, as said below
- boundary: int32 [16, 16, 256], P('vertex'), may hold values from 0 to 4095
- counts: int32 [16, 16], P('vertex'), may hold values from 64 to 256, as said below
- cotangent: bfloat16 [1024, 32768], P('feat', 'vertex'), may hold values from -6 to 6
Outputs:
- activation: bfloat16 [1024, 32768], P('feat', 'vertex')
- neigh_grad: float32 [768, 1024], P('feat', 'vertex')
- self_grad: float32 [768, 1024], P('feat', 'vertex')
- bias_grad: float32 [1024], P('feat')
The draws below stay inside these ranges and needn't reach their ends.
Inputs may be any that keep to these rules, and one draw needn't show every extreme that they name: `counts`: the largest value is reached in every draw. `neighbors`: -1 marks an empty slot; a value v < 4096 is a node of the seed's own partition; v = 4096 + q * 256 + c names slot c of the boundary list from partition q to the seed's partition, with c < counts[q, that partition]. Slot 0 of every seed is not empty.
All inputs are finite; a program needn't handle non-finite values.
Results may differ from the reference program's by a relative error of at most 0.0035.
Values may be sent and summed in bfloat16 or wider, within the bound.
No kernel may reach another device: no remote copies, remote signals or barrier semaphores. Data moves between devices by JAX's collectives and lax.ppermute only.
A program may use at most 64 MiB of HBM per device.

```python
import math
import jax
import jax.numpy as jnp
from jax import lax

F = 768
HID = 1024
K = 25
S_DEV = 2048
NV_DEV = 4096
CAP = 256
NODES = 65536
SEEDS = 32768
N_VERTEX = 16


def shared_counts(key):
    key = jax.random.fold_in(key, 11)
    drawn = jax.random.randint(key, (N_VERTEX, N_VERTEX), CAP // 4, CAP + 1)
    row_ids = jnp.arange(N_VERTEX)[:, None]
    col_ids = jnp.arange(N_VERTEX)[None, :]
    return jnp.where((row_ids == N_VERTEX - 1) & (col_ids == 0), CAP, drawn).astype(jnp.int32)


def draw_counts(key, part):
    return shared_counts(key)


def draw_neighbors(key, part):
    used_counts = shared_counts(key)
    key = jax.random.fold_in(key, 5)
    keys = jax.random.split(key, 5)
    total_rows = N_VERTEX * S_DEV
    owner = jnp.arange(total_rows) // S_DEV
    degree = jax.random.randint(keys[0], (total_rows, 1), 1, K + 1)
    slot_ids = jnp.arange(K)[None, :]
    local_ids = jax.random.randint(keys[1], (total_rows, K), 0, NV_DEV)
    source = jax.random.randint(keys[2], (total_rows, K), 0, N_VERTEX)
    limit = used_counts[source, owner[:, None]]
    within = jax.random.randint(keys[3], (total_rows, K), 0, limit)
    remote_ids = NV_DEV + source * CAP + within
    picker = jax.random.randint(keys[4], (total_rows, K), 0, 2)
    values = jnp.where(picker == 0, local_ids, remote_ids)
    values = jnp.where(slot_ids < degree, values, -1)
    row_ids = jnp.arange(total_rows)[:, None]
    values = jnp.where((row_ids == 0) & (slot_ids == 0), NV_DEV + N_VERTEX * CAP - 1, values)
    values = jnp.where((row_ids == 0) & (slot_ids == K - 1), -1, values)
    return values.T.astype(jnp.int32)


def set_ends(values, stream_key, low, top_value):
    dims = values.shape
    index_at = [jax.random.randint(jax.random.fold_in(stream_key, axis), (), 0, dims[axis]) for axis in range(len(dims))]
    values = values.at[tuple(index_at)].set(low)
    longest = dims.index(max(dims))
    index_at[longest] = (index_at[longest] + 1) % dims[longest]
    return values.at[tuple(index_at)].set(top_value)


def raised(result, stream_key, source, target, shards_of, factor):
    owner, partner = [(jnp.arange(result.shape[axis_at]) // (result.shape[axis_at] // shards_of)).reshape([-1 if axis == axis_at else 1 for axis in range(result.ndim)]) for axis_at in (source, target)]
    chosen = jax.random.permutation(stream_key, shards_of)[partner]
    strong = (owner == chosen) | (owner == (partner + shards_of // 2) % shards_of)
    return jnp.where(strong, factor * result, result)


def steps_of(stream_key, dims, cuts, smallest, high):
    loudness = 1.0
    for dim, shards_of in cuts:
        draws = jax.random.uniform(jax.random.fold_in(jax.random.fold_in(stream_key, 6), dim), (shards_of,), jnp.float32, smallest / len(cuts), high / len(cuts))
        loudness = loudness * jnp.repeat(jnp.exp(draws), dims[dim] // shards_of).reshape((-1,) + (1,) * (len(dims) - 1 - dim))
    return loudness


def scatter_about(stream_key, shape, deviation, bound, pieces=(), kind=jnp.bfloat16):
    result = deviation * jax.random.normal(stream_key, shape, jnp.float32)
    if pieces:
        result = result * steps_of(stream_key, shape, pieces, -0.22, 0.18)
    return jnp.clip(result, -bound, bound).astype(kind)


def bell_draw_with(stream_key, extent, deviation, most, shards, heavy, held_as=jnp.bfloat16):
    values = deviation * jax.random.normal(stream_key, extent, jnp.float32)
    if shards:
        values = values * steps_of(stream_key, extent, shards, -0.22, 0.18)
    return jnp.clip(raised(values, jax.random.fold_in(stream_key, 3), *heavy), -most, most).astype(held_as)


def setup_inputs(seed: int = 0) -> dict:
    key_of = jax.random.split(jax.random.key(seed), 9)
    return {
        "features": scatter_about(key_of[0], (F, NODES), 1.0, 6.0, ((0, 16), (1, 16))),
        "neigh_weight": bell_draw_with(key_of[1], (F, HID), F ** -0.5, 0.3125, ((0, 16),), (0, 1, 16, 2.0)),
        "self_weight": scatter_about(key_of[2], (F, HID), F ** -0.5, 0.21875, ((0, 16),)),
        "bias": jnp.clip(jax.random.uniform(key_of[3], (HID,), jnp.float32, -1.0, 1.0) * steps_of(key_of[3], (HID,), ((0, 16),), -0.4, 0.0), -1.0, 1.0).astype(jnp.bfloat16),
        "neighbors": draw_neighbors(jax.random.fold_in(key_of[8], 71), 0),
        "boundary": set_ends(jax.random.randint(key_of[5], (N_VERTEX, N_VERTEX, CAP), 0, NV_DEV), jax.random.fold_in(key_of[5], 1), 0, NV_DEV - 1).astype(jnp.int32),
        "counts": draw_counts(jax.random.fold_in(key_of[8], 71), 0),
        "cotangent": bell_draw_with(key_of[7], (HID, SEEDS), 1.0, 6.0, ((0, 16), (1, 16)), (1, 0, 16, 2.0)),
    }


def partition(features, neighbors, boundary, counts, part_id):
    local_rows = lax.dynamic_slice_in_dim(features, part_id * NV_DEV, NV_DEV, 0)
    sources = jnp.arange(N_VERTEX, dtype=jnp.int32)[:, None] * NV_DEV
    send_rows = sources + lax.dynamic_index_in_dim(boundary, part_id, 1, keepdims=False)
    used_counts = lax.dynamic_index_in_dim(counts, part_id, 1, keepdims=False)
    usable = jnp.arange(CAP, dtype=jnp.int32)[None, :] < used_counts[:, None]
    remote = jnp.where(usable[:, :, None], features[send_rows], jnp.zeros((), jnp.bfloat16))
    lookup = jnp.concatenate([local_rows, remote.reshape(N_VERTEX * CAP, F), jnp.zeros((1, F), jnp.bfloat16)], axis=0)
    seed_slots = lax.dynamic_slice_in_dim(neighbors, part_id * S_DEV, S_DEV, 0)
    position = jnp.where(seed_slots < 0, NV_DEV + N_VERTEX * CAP, seed_slots).astype(jnp.int32)
    summed = lax.optimization_barrier(jnp.sum(lookup[position].astype(jnp.float32), axis=1))
    degree = lax.optimization_barrier(jnp.sum((seed_slots >= 0).astype(jnp.float32), axis=1))
    neigh_mean = (summed / degree[:, None]).astype(jnp.bfloat16)
    return (neigh_mean, local_rows[:S_DEV])

def reference(features, neigh_weight, self_weight, bias, neighbors, boundary, counts, cotangent):
    features = features.T
    neighbors = neighbors.T
    cotangent = cotangent.T
    neigh_mean, own_rows = lax.map(lambda part_id: partition(features, neighbors, boundary, counts, part_id), jnp.arange(N_VERTEX, dtype=jnp.int32))
    neigh_mean = neigh_mean.reshape(SEEDS, F)
    own_rows = own_rows.reshape(SEEDS, F)
    preact = jnp.dot(neigh_mean, neigh_weight, preferred_element_type=jnp.float32) + jnp.dot(own_rows, self_weight, preferred_element_type=jnp.float32)
    preact = preact + bias.astype(jnp.float32)
    activation = jnp.where(preact > 0, preact, jnp.exp(jnp.minimum(preact, 0.0)) - 1.0).astype(jnp.bfloat16)
    slope = jnp.where(preact > 0, 1.0, jnp.exp(jnp.minimum(preact, 0.0)))
    grad_pre = (cotangent.astype(jnp.float32) * slope).astype(jnp.bfloat16)
    factor = 1.0 / math.sqrt(SEEDS)
    neigh_grad = jnp.dot(neigh_mean.T, grad_pre, preferred_element_type=jnp.float32) * factor
    self_grad = jnp.dot(own_rows.T, grad_pre, preferred_element_type=jnp.float32) * factor
    bias_grad = lax.optimization_barrier(jnp.sum(grad_pre.astype(jnp.float32), axis=0)) * factor
    return (activation.T, neigh_grad, self_grad, bias_grad)
```

```python
import functools
import math

import jax
import jax.numpy as jnp
from jax import lax
from jax.experimental import pallas as pl
from jax.experimental.pallas import tpu as pltpu
from jax.sharding import PartitionSpec as P

LOW = 256
UNROLL = 8
FIRST = 3
PAD = 32
GROUP = 8
VMEM = 60 * 1024 * 1024
NT = (((1,), (1,)), ((), ()))
TN = (((0,), (0,)), ((), ()))


def one_hot(keys, rows):
    width = keys.shape[1]
    wide = jnp.broadcast_to(keys, (16, width)).astype(jnp.bfloat16)
    base = lax.broadcasted_iota(jnp.int32, (rows, width), 0).astype(jnp.float32).astype(jnp.bfloat16)
    base = base.reshape(rows // 16, 16, width)
    hit = base == wide[None]
    return jnp.where(hit, jnp.bfloat16(1), jnp.bfloat16(0)).reshape(rows, width)


def pick_kernel(features_ref, boundary_ref, counts_ref, out_ref, rows_ref):
    columns, nodes = features_ref.shape
    groups = nodes // LOW
    lists, capacity = boundary_ref.shape
    for high in range(groups):
        rows_ref[pl.ds(high * columns, columns), :] = features_ref[:, pl.ds(high * LOW, LOW)]
    slot = lax.broadcasted_iota(jnp.int32, (1, capacity), 1)

    def one_list(p):
        listed = boundary_ref[pl.ds(p, 1), :]
        used = slot < counts_ref[0, p]
        high = jnp.where(used, listed // LOW, -1)
        low = (listed % LOW).astype(jnp.float32)
        found = jnp.dot(rows_ref[...], one_hot(low, LOW), preferred_element_type=jnp.float32)
        total = jnp.zeros((columns, capacity), jnp.float32)
        for group in range(groups):
            total = total + jnp.where(high == group, found[group * columns:(group + 1) * columns], 0.0)
        out_ref[p] = total.astype(out_ref.dtype)

    def some_lists(i, carry):
        for k in range(4):
            one_list(4 * i + k)
        return carry

    lax.fori_loop(0, lists // 4, some_lists, 0)


def pick(features, boundary, counts):
    columns, nodes = features.shape
    lists, capacity = boundary.shape
    vm = pl.BlockSpec(memory_space=pltpu.VMEM)
    return pl.pallas_call(
        pick_kernel,
        out_shape=jax.ShapeDtypeStruct((lists, columns, capacity), jnp.bfloat16),
        in_specs=[vm, vm, pl.BlockSpec(memory_space=pltpu.SMEM)],
        out_specs=vm,
        scratch_shapes=[pltpu.VMEM((columns * nodes // LOW, LOW), jnp.bfloat16)],
        compiler_params=pltpu.CompilerParams(vmem_limit_bytes=VMEM),
        name="pick",
    )(features, boundary, counts)


def pack_kernel(parity_ref, features_ref, neigh_weight_ref, self_weight_ref, cotangent_ref, bias_ref,
                inputs_ref, traded_ref):
    shares, _, width = inputs_ref.shape
    half = features_ref.shape[1] // 2
    wide = (width - half) // 2
    for share in range(shares):
        inputs_ref[share, :, pl.ds(0, half)] = features_ref[:, pl.ds((share % 2) * half, half)]
        at = pl.ds((share // 2) * wide, wide)
        inputs_ref[share, :, pl.ds(half, wide)] = neigh_weight_ref[:, at]
        inputs_ref[share, :, pl.ds(half + wide, wide)] = self_weight_ref[:, at]
    traded_ref[:, pl.ds(0, half)] = cotangent_ref[:, pl.ds(pl.multiple_of((1 - parity_ref[0]) * half, half), half)]
    hidden, rest = traded_ref.shape[0], traded_ref.shape[1] - half
    traded_ref[:, pl.ds(half, rest)] = jnp.broadcast_to(bias_ref[...], (hidden, rest))


def pack(parity, features, neigh_weight, self_weight, cotangent, bias, shares):
    columns = features.shape[0]
    hidden, seed_count = cotangent.shape
    half = seed_count // 2
    whole = lambda i: (0, 0)
    return pl.pallas_call(
        pack_kernel,
        grid=(1,),
        out_shape=(jax.ShapeDtypeStruct((shares, columns, half + 4 * hidden), jnp.bfloat16),
                   jax.ShapeDtypeStruct((hidden, half + 128), jnp.bfloat16)),
        in_specs=[pl.BlockSpec(memory_space=pltpu.SMEM),
                  pl.BlockSpec((columns, seed_count), whole),
                  pl.BlockSpec(neigh_weight.shape, whole),
                  pl.BlockSpec(self_weight.shape, whole),
                  pl.BlockSpec(cotangent.shape, whole),
                  pl.BlockSpec(bias.shape, whole)],
        out_specs=(pl.BlockSpec((shares, columns, half + 4 * hidden), lambda i: (0, 0, 0)),
                   pl.BlockSpec((hidden, half + 128), whole)),
        compiler_params=pltpu.CompilerParams(vmem_limit_bytes=VMEM),
        name="pack",
    )(parity, features, neigh_weight, self_weight, cotangent, bias)


def fill_table(first_group, groups, rank_ref, low_ref, store):
    def pairs(i, carry):
        for unrolled in range(UNROLL):
            pair = i * UNROLL + unrolled
            found = []
            for k in range(2):
                group = first_group + 2 * pair + k
                left = one_hot(rank_ref[pl.ds(group, 1), :], rank_ref.shape[1])
                right = one_hot(low_ref[pl.ds(group, 1), :], LOW)
                table = lax.dot_general(left, right, NT, preferred_element_type=jnp.float32)
                found.append(table.reshape(table.shape[0] // GROUP, GROUP, LOW))
            rows = pl.ds(pl.multiple_of(pair * 2 * GROUP, 2 * GROUP), 2 * GROUP)
            store(rows, jnp.concatenate(found, axis=1).astype(jnp.bfloat16))
        return carry

    lax.fori_loop(0, groups // 2 // UNROLL, pairs, 0)


def table_kernel(neighbors_ref, features_ref, remote_ref, local_ref, rank_ref, low_ref, local_table_ref):
    slot_count, seed_count = neighbors_ref.shape
    group_count = seed_count // GROUP
    rows, half = local_table_ref.shape
    highs = half // LOW
    step = pl.program_id(0)

    @pl.when(step == 0)
    def _():
        ranks = []
        lows = []
        for member in range(GROUP):
            value = neighbors_ref[:, pl.ds(member * group_count, group_count)]
            value = jnp.concatenate(
                [value, jnp.full((PAD - slot_count, group_count), -1, jnp.int32)], axis=0)
            rank = jnp.where(value < 0, -1, (value // LOW) * GROUP + member)
            ranks.append(rank.astype(jnp.float32))
            lows.append((value % LOW).astype(jnp.float32))
        rank_ref[...] = jnp.concatenate(ranks, axis=0).T
        low_ref[...] = jnp.concatenate(lows, axis=0).T

    def store(at, table):
        for high in range(highs):
            local_table_ref[at, pl.ds(high * LOW, LOW)] = table[high]
            remote_ref[at, pl.ds(high * LOW, LOW)] = table[highs + high]

    groups = rows // GROUP
    fill_table(step * groups, groups, rank_ref, low_ref, store)
    local_ref[...] = lax.dot_general(
        local_table_ref[...], features_ref[...], NT, preferred_element_type=jnp.float32)


def first_tables(neighbors, features, blocks, rows=256):
    slot_count, seed_count = neighbors.shape
    columns, nodes = features.shape
    group_count = seed_count // GROUP
    keys = jax.ShapeDtypeStruct((group_count, GROUP * PAD), jnp.float32)
    whole = lambda i: (0, 0)
    return pl.pallas_call(
        table_kernel,
        grid=(blocks,),
        out_shape=(jax.ShapeDtypeStruct((blocks * rows, nodes), jnp.bfloat16),
                   jax.ShapeDtypeStruct((blocks * rows, columns), jnp.float32), keys, keys),
        in_specs=[pl.BlockSpec((slot_count, seed_count), whole), pl.BlockSpec((columns, nodes), whole)],
        out_specs=(pl.BlockSpec((rows, nodes), lambda i: (i, 0)),
                   pl.BlockSpec((rows, columns), lambda i: (i, 0)),
                   pl.BlockSpec(keys.shape, whole), pl.BlockSpec(keys.shape, whole)),
        scratch_shapes=[pltpu.VMEM((rows, nodes), jnp.bfloat16)],
        compiler_params=pltpu.CompilerParams(vmem_limit_bytes=VMEM),
        name="first_tables",
    )(neighbors, features)


def mean_kernel(rows, remote_ref, incoming_ref, local_ref, rank_ref, low_ref, neighbors_ref, features_ref,
                out_ref, lookup_ref, sum_ref, table_ref, held_ref, sems):
    sources, columns, capacity = incoming_ref.shape
    nodes = features_ref.shape[1]
    seed_count = sum_ref.shape[0]
    group_count = seed_count // GROUP
    blocks = held_ref.shape[0]
    copies = [
        pltpu.make_async_copy(remote_ref.at[pl.ds(k * rows, rows), :], held_ref.at[k], sems.at[k])
        for k in range(blocks)]
    for copy in copies:
        copy.start()
    lookup_ref[:, pl.ds(0, nodes)] = features_ref[...]
    for source in range(sources):
        lookup_ref[:, pl.ds(nodes + source * capacity, capacity)] = incoming_ref[source]

    def store(at, table):
        for high in range(table.shape[0]):
            table_ref[at, pl.ds(high * LOW, LOW)] = table[high]

    def build(k, carry):
        fill_table(k * (rows // GROUP), rows // GROUP, rank_ref, low_ref, store)
        sum_ref[pl.ds(pl.multiple_of(k * rows, rows), rows), pl.ds(0, columns)] = lax.dot_general(
            table_ref[...], lookup_ref[...], NT, preferred_element_type=jnp.float32)
        return carry

    lax.fori_loop(blocks, seed_count // rows, build, 0)
    for k in range(blocks):
        copies[k].wait()
        at = pl.ds(k * rows, rows)
        sum_ref[at, pl.ds(0, columns)] = local_ref[at, :] + lax.dot_general(
            held_ref[k], lookup_ref[:, nodes:], NT, preferred_element_type=jnp.float32)

    degree = jnp.sum(jnp.where(neighbors_ref[...] >= 0, 1.0, 0.0), axis=0, keepdims=True)
    shares, _, half = out_ref.shape
    for member in range(GROUP):
        mine = sum_ref[pl.ds(member, group_count, stride=GROUP), :].T[:columns]
        start = member * group_count
        mine = mine / degree[:, start:start + group_count]
        mine = mine.astype(jnp.bfloat16)
        for share in range(start // half, shares, 2):
            out_ref[share, :, pl.ds(start % half, group_count)] = mine


def neighbor_mean(remote, incoming, local, rank, low, neighbors, features, shares, rows=256):
    slot_count, seed_count = neighbors.shape
    columns, nodes = features.shape
    sources, _, capacity = incoming.shape
    blocks = remote.shape[0] // rows
    lookup_width = nodes + sources * capacity
    vm = pl.BlockSpec(memory_space=pltpu.VMEM)
    return pl.pallas_call(
        functools.partial(mean_kernel, rows),
        out_shape=jax.ShapeDtypeStruct((shares, columns, seed_count // 2), jnp.bfloat16),
        in_specs=[pl.BlockSpec(memory_space=pl.ANY)] + [vm] * 6,
        out_specs=vm,
        scratch_shapes=[pltpu.VMEM((columns, lookup_width), jnp.bfloat16),
                        pltpu.VMEM((seed_count, 128), jnp.float32),
                        pltpu.VMEM((rows, lookup_width), jnp.bfloat16),
                        pltpu.VMEM((blocks, rows, nodes), jnp.bfloat16),
                        pltpu.SemaphoreType.DMA((blocks,))],
        compiler_params=pltpu.CompilerParams(vmem_limit_bytes=VMEM),
        name="mean",
    )(remote, incoming, local, rank, low, neighbors, features)


def layer_kernel(parity_ref, own_ref, mean_ref, neigh_weight_ref, self_weight_ref, bias_ref, cotangent_ref,
                 traded_ref, traded_bias_ref, kept_ref, sent_ref, grad_ref, total_ref, sums_ref):
    step = pl.program_id(0)
    odd = parity_ref[0] == 1
    hidden = cotangent_ref.shape[0]

    @pl.when(step == 0)
    def _():
        total_ref[...] = jnp.zeros_like(total_ref)
        sums_ref[...] = jnp.zeros_like(sums_ref)

    def ordered(mine, other):
        return jnp.concatenate([jnp.where(odd, other, mine), jnp.where(odd, mine, other)], axis=0)

    bias = ordered(bias_ref[...].astype(jnp.float32), traded_bias_ref[:, :1].astype(jnp.float32))
    cotangent = ordered(cotangent_ref[...].astype(jnp.float32), traded_ref[...].astype(jnp.float32))
    preact = (
        lax.dot_general(neigh_weight_ref[...], mean_ref[...], TN, preferred_element_type=jnp.float32)
        + lax.dot_general(self_weight_ref[...], own_ref[...], TN, preferred_element_type=jnp.float32)
        + bias
    )
    decay = jnp.exp(jnp.minimum(preact, 0.0))
    activation = jnp.where(preact > 0, preact, decay - 1.0)
    kept_ref[...] = jnp.where(odd, activation[hidden:], activation[:hidden]).astype(jnp.bfloat16)
    sent_ref[...] = jnp.where(odd, activation[:hidden], activation[hidden:]).astype(jnp.bfloat16)
    slope = jnp.where(preact > 0, 1.0, decay)
    grad_pre = (cotangent * slope).astype(jnp.bfloat16)
    pair = 2 * hidden
    total_ref[:, pl.ds(0, pair)] += lax.dot_general(
        mean_ref[...], grad_pre, NT, preferred_element_type=jnp.float32)
    total_ref[:, pl.ds(pair, pair)] += lax.dot_general(
        own_ref[...], grad_pre, NT, preferred_element_type=jnp.float32)
    sums_ref[...] += lax.dot_general(
        jnp.ones((sums_ref.shape[0], grad_pre.shape[1]), jnp.bfloat16), grad_pre, NT,
        preferred_element_type=jnp.float32)

    @pl.when(step == pl.num_programs(0) - 1)
    def _():
        shares, rows, _ = grad_ref.shape
        columns = total_ref.shape[0] // shares
        sums = sums_ref[...]
        high = sums.astype(jnp.bfloat16).astype(jnp.float32)
        row = lax.broadcasted_iota(jnp.int32, sums.shape, 0)
        extra = jnp.where(row == 0, high, jnp.where(row == 1, sums - high, 0.0))
        extra = jnp.concatenate([extra, jnp.zeros_like(extra)], axis=1).astype(jnp.bfloat16)
        for share in range(shares):
            grad_ref[share, pl.ds(0, columns), :] = total_ref[
                pl.ds(share * columns, columns), :].astype(jnp.bfloat16)
            grad_ref[share, pl.ds(columns, rows - columns), :] = extra


def layer(parity, inputs, mean, bias, cotangent, traded, shares, block=512):
    features, half = mean.shape
    hidden = cotangent.shape[0]
    pair = 2 * hidden
    extra = 16
    blocks = half // block
    whole = lambda i, parity: (0, 0)
    part = lambda i, parity: (0, i)
    grads = (shares, features // shares + extra, 2 * pair)
    return pl.pallas_call(
        layer_kernel,
        grid_spec=pltpu.PrefetchScalarGridSpec(
            num_scalar_prefetch=1,
            grid=(blocks,),
            in_specs=[pl.BlockSpec((features, block), part),
                      pl.BlockSpec((features, block), part),
                      pl.BlockSpec((features, pair), lambda i, parity: (0, half // pair)),
                      pl.BlockSpec((features, pair), lambda i, parity: (0, half // pair + 1)),
                      pl.BlockSpec((hidden, 1), whole),
                      pl.BlockSpec((hidden, block), lambda i, parity: (0, i + parity[0] * blocks)),
                      pl.BlockSpec((hidden, block), part),
                      pl.BlockSpec((hidden, 128), lambda i, parity: (0, half // 128))],
            out_specs=(pl.BlockSpec((hidden, block), part),
                       pl.BlockSpec((hidden, block), part),
                       pl.BlockSpec(grads, lambda i, parity: (0, 0, 0))),
            scratch_shapes=[pltpu.VMEM((features, 2 * pair), jnp.float32),
                            pltpu.VMEM((extra, pair), jnp.float32)]),
        out_shape=(jax.ShapeDtypeStruct((hidden, half), jnp.bfloat16),
                   jax.ShapeDtypeStruct((hidden, half), jnp.bfloat16),
                   jax.ShapeDtypeStruct(grads, jnp.bfloat16)),
        compiler_params=pltpu.CompilerParams(vmem_limit_bytes=VMEM),
        name="layer",
    )(parity, inputs, mean, inputs, inputs, bias, cotangent, traded, traded)


def body(features, neigh_weight, self_weight, bias, neighbors, boundary, counts, cotangent):
    columns, nodes = features.shape
    partitions = lax.axis_size("vertex")
    shares = lax.axis_size("feat")
    seed_count = neighbors.shape[1]
    hidden = cotangent.shape[0]
    pair = 2 * hidden
    odd = lax.axis_index("feat") % 2
    parity = odd.astype(jnp.int32).reshape(1)
    bias = bias.reshape(hidden, 1)
    trade = [(f, f ^ 1) for f in range(shares)]

    outgoing = pick(features, boundary[0], counts)
    incoming = lax.all_to_all(outgoing, "vertex", split_axis=0, concat_axis=0, tiled=True)
    _, late = lax.optimization_barrier((outgoing, parity))
    inputs, traded = pack(late, features, neigh_weight, self_weight, cotangent, bias, shares)
    remote, local, rank, low = first_tables(neighbors, features, FIRST)
    inputs, _ = lax.optimization_barrier((inputs, local))
    inputs = lax.all_to_all(inputs, "feat", split_axis=0, concat_axis=0, tiled=True)
    inputs = inputs.reshape(shares * columns, inputs.shape[2])
    traded = lax.ppermute(traded, "feat", trade)
    mean = neighbor_mean(remote, incoming, local, rank, low, neighbors, features, shares)
    mean = lax.all_to_all(mean, "feat", split_axis=0, concat_axis=0, tiled=True)
    mean = mean.reshape(shares * columns, mean.shape[2])
    kept, sent, grad = layer(parity, inputs, mean, bias, cotangent, traded, shares)
    grad = lax.all_to_all(grad, "vertex", split_axis=0, concat_axis=0, tiled=True)
    other = lax.ppermute(sent, "feat", trade)
    activation = jnp.concatenate(
        [jnp.where(odd == 1, other, kept), jnp.where(odd == 1, kept, other)], axis=1)

    factor = 1.0 / math.sqrt(seed_count * partitions)
    grad = jnp.sum(grad.astype(jnp.float32), axis=0) * factor
    bias_sum = grad[columns, :pair] + grad[columns + 1, :pair]
    neigh, own = grad[:columns, :pair], grad[:columns, pair:]
    even_part = jnp.concatenate([neigh[:, :hidden], own[:, :hidden]], axis=1)
    odd_part = jnp.concatenate([neigh[:, hidden:], own[:, hidden:]], axis=1)
    pieces = []
    for k in range(2):
        route = [(v * shares + f, (2 * (f // 2) + (f % 2 ^ k)) * shares + v)
                 for v in range(partitions) for f in range(shares)]
        piece = jnp.where((odd ^ k) == 1, odd_part, even_part)
        pieces.append(lax.ppermute(piece, ("vertex", "feat"), route))
    grad = pieces[0] + pieces[1]
    mine = jnp.where(odd == 1, bias_sum[hidden:], bias_sum[:hidden])
    theirs = jnp.where(odd == 1, bias_sum[:hidden], bias_sum[hidden:])
    bias_out = mine + lax.ppermute(theirs, "feat", trade)
    return activation, grad[:, :hidden], grad[:, hidden:], bias_out


def solution(mesh):
    placed = (
        P("feat", "vertex"),
        P("feat", None),
        P("feat", None),
        P("feat"),
        P(None, "vertex"),
        P("vertex", None, None),
        P("vertex", None),
        P("feat", "vertex"),
    )
    return jax.shard_map(
        body,
        mesh=mesh,
        in_specs=placed,
        out_specs=(P("feat", "vertex"), P("feat", "vertex"), P("feat", "vertex"), P("feat")),
        check_vma=False,
    )
```

```python
import functools
import math

import jax
import jax.numpy as jnp
from jax import lax
from jax.experimental import pallas as pl
from jax.experimental.pallas import tpu as pltpu
from jax.sharding import PartitionSpec as P

LOW = 256
ONES = jnp.float8_e4m3fn
UNROLL = 8
FIRST = 4
RADIX = 4
PAD = 32
GROUP = 8
EXTRA = 16
VMEM = 60 * 1024 * 1024
NT = (((1,), (1,)), ((), ()))
TN = (((0,), (0,)), ((), ()))


def one_hot(keys, rows):
    width = keys.shape[1]
    wide = jnp.broadcast_to(keys, (16, width)).astype(jnp.bfloat16)
    base = lax.broadcasted_iota(jnp.int32, (rows, width), 0).astype(jnp.float32).astype(jnp.bfloat16)
    base = base.reshape(rows // 16, 16, width)
    hit = base == wide[None]
    return jnp.where(hit, jnp.bfloat16(1), jnp.bfloat16(0)).reshape(rows, width)


def relative(place, j, k):
    return ((place // RADIX + j) % RADIX) * RADIX + (place % RADIX + k) % RADIX


def pick_kernel(place_ref, features_ref, boundary_ref, counts_ref, *refs):
    out_refs, rows_ref = refs[:RADIX], refs[RADIX]
    columns, nodes = features_ref.shape
    groups = nodes // LOW
    capacity = boundary_ref.shape[1]
    for high in range(groups):
        rows_ref[pl.ds(high * columns, columns), :] = features_ref[:, pl.ds(high * LOW, LOW)]
    slot = lax.broadcasted_iota(jnp.int32, (1, capacity), 1)
    for k in range(RADIX):
        for j in range(RADIX):
            p = relative(place_ref[0], j, k)
            listed = boundary_ref[pl.ds(p, 1), :]
            used = slot < counts_ref[0, p]
            high = jnp.where(used, listed >> 8, -1)
            low = (listed & (LOW - 1)).astype(jnp.float32)
            found = jnp.dot(rows_ref[...], one_hot(low, LOW), preferred_element_type=jnp.float32)
            total = jnp.zeros((columns, capacity), jnp.float32)
            for group in range(groups):
                total = total + jnp.where(high == group, found[group * columns:(group + 1) * columns], 0.0)
            out_refs[k][j] = total.astype(jnp.bfloat16)


def pick(place, features, boundary, counts):
    columns, nodes = features.shape
    capacity = boundary.shape[1]
    vm = pl.BlockSpec(memory_space=pltpu.VMEM)
    sm = pl.BlockSpec(memory_space=pltpu.SMEM)
    return pl.pallas_call(
        pick_kernel,
        out_shape=(jax.ShapeDtypeStruct((RADIX, columns, capacity), jnp.bfloat16),) * RADIX,
        in_specs=[sm, vm, vm, sm],
        out_specs=(vm,) * RADIX,
        scratch_shapes=[pltpu.VMEM((columns * nodes // LOW, LOW), jnp.bfloat16)],
        compiler_params=pltpu.CompilerParams(vmem_limit_bytes=VMEM),
        name="pick",
    )(place, features, boundary, counts)


def regroup_kernel(*refs):
    in_refs, out_refs = refs[:RADIX], refs[RADIX:]
    for j, out_ref in enumerate(out_refs, 1):
        for k, in_ref in enumerate(in_refs):
            out_ref[k] = in_ref[j]


def regroup(pieces):
    vm = pl.BlockSpec(memory_space=pltpu.VMEM)
    return pl.pallas_call(
        regroup_kernel,
        out_shape=(jax.ShapeDtypeStruct(pieces[0].shape, jnp.bfloat16),) * (RADIX - 1),
        in_specs=[vm] * RADIX,
        out_specs=(vm,) * (RADIX - 1),
        name="regroup",
    )(*pieces)


def pack_kernel(parity_ref, features_ref, neigh_weight_ref, self_weight_ref, cotangent_ref, bias_ref,
                inputs_ref, traded_ref):
    shares, _, width = inputs_ref.shape
    half = features_ref.shape[1] // 2
    wide = (width - half) // 2
    for share in range(shares):
        inputs_ref[share, :, pl.ds(0, half)] = features_ref[:, pl.ds((share % 2) * half, half)]
        at = pl.ds((share // 2) * wide, wide)
        inputs_ref[share, :, pl.ds(half, wide)] = neigh_weight_ref[:, at]
        inputs_ref[share, :, pl.ds(half + wide, wide)] = self_weight_ref[:, at]
    hidden = cotangent_ref.shape[0]
    traded_ref[pl.ds(0, hidden), :] = cotangent_ref[
        :, pl.ds(pl.multiple_of((1 - parity_ref[0]) * half, half), half)]
    bias = jnp.concatenate([bias_ref[...], jnp.zeros((1, half - hidden), jnp.bfloat16)], axis=1)
    traded_ref[pl.ds(hidden, EXTRA), :] = jnp.broadcast_to(bias.astype(jnp.float32), (EXTRA, half)).astype(jnp.bfloat16)


def pack(parity, features, neigh_weight, self_weight, cotangent, bias, shares):
    columns = features.shape[0]
    hidden, seed_count = cotangent.shape
    half = seed_count // 2
    whole = lambda i: (0, 0)
    return pl.pallas_call(
        pack_kernel,
        grid=(1,),
        out_shape=(jax.ShapeDtypeStruct((shares, columns, half + 4 * hidden), jnp.bfloat16),
                   jax.ShapeDtypeStruct((hidden + EXTRA, half), jnp.bfloat16)),
        in_specs=[pl.BlockSpec(memory_space=pltpu.SMEM),
                  pl.BlockSpec((columns, seed_count), whole),
                  pl.BlockSpec(neigh_weight.shape, whole),
                  pl.BlockSpec(self_weight.shape, whole),
                  pl.BlockSpec(cotangent.shape, whole),
                  pl.BlockSpec(bias.shape, whole)],
        out_specs=(pl.BlockSpec((shares, columns, half + 4 * hidden), lambda i: (0, 0, 0)),
                   pl.BlockSpec((hidden + EXTRA, half), whole)),
        compiler_params=pltpu.CompilerParams(vmem_limit_bytes=VMEM),
        name="pack",
    )(parity, features, neigh_weight, self_weight, cotangent, bias)


def fill_table(first_group, groups, rank_ref, low_ref, store):
    def pairs(i, carry):
        for unrolled in range(UNROLL):
            pair = i * UNROLL + unrolled
            found = []
            for k in range(2):
                group = first_group + 2 * pair + k
                left = one_hot(rank_ref[pl.ds(group, 1), :], rank_ref.shape[1]).astype(ONES)
                right = one_hot(low_ref[pl.ds(group, 1), :], LOW).astype(ONES)
                table = lax.dot_general(left, right, NT, preferred_element_type=jnp.float32)
                found.append(table.reshape(table.shape[0] // GROUP, GROUP, LOW))
            rows = pl.ds(pl.multiple_of(pair * 2 * GROUP, 2 * GROUP), 2 * GROUP)
            store(rows, jnp.concatenate(found, axis=1).astype(jnp.bfloat16))
        return carry

    lax.fori_loop(0, groups // 2 // UNROLL, pairs, 0)


def table_kernel(neighbors_ref, features_ref, remote_ref, local_ref, rank_ref, low_ref, local_table_ref):
    slot_count, seed_count = neighbors_ref.shape
    group_count = seed_count // GROUP
    rows, half = local_table_ref.shape
    highs = half // LOW
    step = pl.program_id(0)

    @pl.when(step == 0)
    def _():
        ranks = []
        lows = []
        for member in range(GROUP):
            value = neighbors_ref[:, pl.ds(member * group_count, group_count)]
            value = jnp.concatenate(
                [value, jnp.full((PAD - slot_count, group_count), -1, jnp.int32)], axis=0)
            rank = jnp.where(value < 0, -1, (value >> 8) * GROUP + member)
            ranks.append(rank.astype(jnp.float32))
            lows.append((value & (LOW - 1)).astype(jnp.float32))
        rank_ref[...] = jnp.concatenate(ranks, axis=0).T
        low_ref[...] = jnp.concatenate(lows, axis=0).T

    def store(at, table):
        for high in range(highs):
            local_table_ref[at, pl.ds(high * LOW, LOW)] = table[high]
            remote_ref[at, pl.ds(high * LOW, LOW)] = table[highs + high]

    groups = rows // GROUP
    fill_table(step * groups, groups, rank_ref, low_ref, store)
    local_ref[...] = lax.dot_general(
        local_table_ref[...], features_ref[...], NT, preferred_element_type=jnp.float32)


def first_tables(neighbors, features, blocks, rows=256):
    slot_count, seed_count = neighbors.shape
    columns, nodes = features.shape
    group_count = seed_count // GROUP
    keys = jax.ShapeDtypeStruct((group_count, GROUP * PAD), jnp.float32)
    whole = lambda i: (0, 0)
    return pl.pallas_call(
        table_kernel,
        grid=(blocks,),
        out_shape=(jax.ShapeDtypeStruct((blocks * rows, nodes), jnp.bfloat16),
                   jax.ShapeDtypeStruct((blocks * rows, columns), jnp.float32), keys, keys),
        in_specs=[pl.BlockSpec((slot_count, seed_count), whole), pl.BlockSpec((columns, nodes), whole)],
        out_specs=(pl.BlockSpec((rows, nodes), lambda i: (i, 0)),
                   pl.BlockSpec((rows, columns), lambda i: (i, 0)),
                   pl.BlockSpec(keys.shape, whole), pl.BlockSpec(keys.shape, whole)),
        scratch_shapes=[pltpu.VMEM((rows, nodes), jnp.bfloat16)],
        compiler_params=pltpu.CompilerParams(vmem_limit_bytes=VMEM),
        name="first_tables",
    )(neighbors, features)


def mean_kernel(rows, place_ref, remote_ref, near_refs, far_refs, local_ref, rank_ref, low_ref, neighbors_ref,
                features_ref, out_ref, lookup_ref, sum_ref, table_ref, held_ref, sems):
    _, columns, capacity = near_refs[0].shape
    nodes = features_ref.shape[1]
    seed_count = sum_ref.shape[0]
    group_count = seed_count // GROUP
    blocks = held_ref.shape[0]
    copies = [
        pltpu.make_async_copy(remote_ref.at[pl.ds(k * rows, rows), :], held_ref.at[k], sems.at[k])
        for k in range(blocks)]
    for copy in copies:
        copy.start()
    lookup_ref[:, pl.ds(0, nodes)] = features_ref[...]
    for j in range(RADIX):
        for k in range(RADIX):
            source = relative(place_ref[0], RADIX - j, RADIX - k)
            at = pl.ds(pl.multiple_of(nodes + source * capacity, capacity), capacity)
            lookup_ref[:, at] = near_refs[k][0] if j == 0 else far_refs[j - 1][k]

    def store(at, table):
        for high in range(table.shape[0]):
            table_ref[at, pl.ds(high * LOW, LOW)] = table[high]

    def build(k, carry):
        fill_table(k * (rows // GROUP), rows // GROUP, rank_ref, low_ref, store)
        sum_ref[pl.ds(pl.multiple_of(k * rows, rows), rows), pl.ds(0, columns)] = lax.dot_general(
            table_ref[...], lookup_ref[...], NT, preferred_element_type=jnp.float32)
        return carry

    lax.fori_loop(blocks, seed_count // rows, build, 0)
    for k in range(blocks):
        copies[k].wait()
        at = pl.ds(k * rows, rows)
        sum_ref[at, pl.ds(0, columns)] = local_ref[at, :] + lax.dot_general(
            held_ref[k], lookup_ref[:, nodes:], NT, preferred_element_type=jnp.float32)

    degree = jnp.sum(jnp.where(neighbors_ref[...] >= 0, 1.0, 0.0), axis=0, keepdims=True)
    shares, _, half = out_ref.shape
    for member in range(GROUP):
        mine = sum_ref[pl.ds(member, group_count, stride=GROUP), :].T[:columns]
        start = member * group_count
        mine = mine / degree[:, start:start + group_count]
        mine = mine.astype(jnp.bfloat16)
        for share in range(start // half, shares, 2):
            out_ref[share, :, pl.ds(start % half, group_count)] = mine


def neighbor_mean(place, remote, near, far, local, rank, low, neighbors, features, shares, rows=256):
    slot_count, seed_count = neighbors.shape
    columns, nodes = features.shape
    capacity = near[0].shape[2]
    blocks = remote.shape[0] // rows
    lookup_width = nodes + RADIX * RADIX * capacity
    vm = pl.BlockSpec(memory_space=pltpu.VMEM)

    def kernel(place_ref, remote_ref, *refs):
        mean_kernel(rows, place_ref, remote_ref, refs[:RADIX], refs[RADIX:2 * RADIX - 1], *refs[2 * RADIX - 1:])

    return pl.pallas_call(
        kernel,
        out_shape=jax.ShapeDtypeStruct((shares, columns, seed_count // 2), jnp.bfloat16),
        in_specs=[pl.BlockSpec(memory_space=pltpu.SMEM), pl.BlockSpec(memory_space=pl.ANY)]
        + [vm] * (2 * RADIX - 1 + 5),
        out_specs=vm,
        scratch_shapes=[pltpu.VMEM((columns, lookup_width), jnp.bfloat16),
                        pltpu.VMEM((seed_count, 128), jnp.float32),
                        pltpu.VMEM((rows, lookup_width), jnp.bfloat16),
                        pltpu.VMEM((blocks, rows, nodes), jnp.bfloat16),
                        pltpu.SemaphoreType.DMA((blocks,))],
        compiler_params=pltpu.CompilerParams(vmem_limit_bytes=VMEM),
        name="mean",
    )(place, remote, *near, *far, local, rank, low, neighbors, features)


def layer_kernel(parity_ref, own_ref, mean_ref, neigh_weight_ref, self_weight_ref, bias_ref, cotangent_ref,
                 traded_ref, traded_bias_ref, kept_ref, sent_ref, grad_ref, total_ref, sums_ref):
    step = pl.program_id(0)
    odd = parity_ref[0] == 1
    hidden = cotangent_ref.shape[0]

    @pl.when(step == 0)
    def _():
        total_ref[...] = jnp.zeros_like(total_ref)
        sums_ref[...] = jnp.zeros_like(sums_ref)

    def ordered(mine, other):
        return jnp.concatenate([jnp.where(odd, other, mine), jnp.where(odd, mine, other)], axis=0)

    mine = bias_ref[...].astype(jnp.float32)
    theirs = traded_bias_ref[:1, :hidden].astype(jnp.float32)
    bias = jnp.concatenate([jnp.where(odd, theirs, mine), jnp.where(odd, mine, theirs)], axis=1)
    row = lax.broadcasted_iota(jnp.int32, (EXTRA, 2 * hidden), 0)
    bias = jnp.where(row == 0, bias, 0.0).astype(jnp.bfloat16)
    ones = jnp.ones((EXTRA, own_ref.shape[1]), jnp.bfloat16)
    cotangent = ordered(cotangent_ref[...].astype(jnp.float32), traded_ref[...].astype(jnp.float32))
    preact = (
        lax.dot_general(neigh_weight_ref[...], mean_ref[...], TN, preferred_element_type=jnp.float32)
        + lax.dot_general(self_weight_ref[...], own_ref[...], TN, preferred_element_type=jnp.float32)
        + lax.dot_general(bias, ones, TN, preferred_element_type=jnp.float32)
    )
    decay = jnp.exp(jnp.minimum(preact, 0.0))
    activation = jnp.where(preact > 0, preact, decay - 1.0)
    kept_ref[...] = jnp.where(odd, activation[hidden:], activation[:hidden]).astype(jnp.bfloat16)
    sent_ref[...] = jnp.where(odd, activation[:hidden], activation[hidden:]).astype(jnp.bfloat16)
    slope = jnp.where(preact > 0, 1.0, decay)
    grad_pre = (cotangent * slope).astype(jnp.bfloat16)
    first, second = grad_pre[:hidden], grad_pre[hidden:]
    blank = jnp.zeros_like(first)
    for_neigh = jnp.concatenate([first, blank, second, blank], axis=0)
    for_own = jnp.concatenate([blank, first, blank, second], axis=0)
    total_ref[...] += (
        lax.dot_general(mean_ref[...], for_neigh, NT, preferred_element_type=jnp.float32)
        + lax.dot_general(own_ref[...], for_own, NT, preferred_element_type=jnp.float32))
    sums_ref[...] += lax.dot_general(ones, for_neigh, NT, preferred_element_type=jnp.float32)

    @pl.when(step == pl.num_programs(0) - 1)
    def _():
        chunks, rows, width = grad_ref.shape
        columns = rows - EXTRA
        sums = sums_ref[...]
        high = sums.astype(jnp.bfloat16).astype(jnp.float32)
        row = lax.broadcasted_iota(jnp.int32, sums.shape, 0)
        extra = jnp.where(row == 0, high, jnp.where(row == 1, sums - high, 0.0)).astype(jnp.bfloat16)
        for chunk in range(chunks):
            at = pl.ds((chunk % 2) * width, width)
            grad_ref[chunk, pl.ds(0, columns), :] = total_ref[
                pl.ds((chunk // 2) * columns, columns), at].astype(jnp.bfloat16)
            grad_ref[chunk, pl.ds(columns, EXTRA), :] = extra[:, (chunk % 2) * width:(chunk % 2 + 1) * width]


def layer(parity, inputs, mean, bias, cotangent, traded, shares, block=512):
    features, half = mean.shape
    hidden = cotangent.shape[0]
    pair = 2 * hidden
    blocks = half // block
    whole = lambda i, parity: (0, 0)
    part = lambda i, parity: (0, i)
    grads = (2 * shares, features // shares + EXTRA, pair)
    return pl.pallas_call(
        layer_kernel,
        grid_spec=pltpu.PrefetchScalarGridSpec(
            num_scalar_prefetch=1,
            grid=(blocks,),
            in_specs=[pl.BlockSpec((features, block), part),
                      pl.BlockSpec((features, block), part),
                      pl.BlockSpec((features, pair), lambda i, parity: (0, half // pair)),
                      pl.BlockSpec((features, pair), lambda i, parity: (0, half // pair + 1)),
                      pl.BlockSpec((1, hidden), whole),
                      pl.BlockSpec((hidden, block), lambda i, parity: (0, i + parity[0] * blocks)),
                      pl.BlockSpec((hidden, block), part),
                      pl.BlockSpec((EXTRA, 128), lambda i, parity: (hidden // EXTRA, 0))],
            out_specs=(pl.BlockSpec((hidden, block), part),
                       pl.BlockSpec((hidden, block), part),
                       pl.BlockSpec(grads, lambda i, parity: (0, 0, 0))),
            scratch_shapes=[pltpu.VMEM((features, 2 * pair), jnp.float32),
                            pltpu.VMEM((EXTRA, 2 * pair), jnp.float32)]),
        out_shape=(jax.ShapeDtypeStruct((hidden, half), jnp.bfloat16),
                   jax.ShapeDtypeStruct((hidden, half), jnp.bfloat16),
                   jax.ShapeDtypeStruct(grads, jnp.bfloat16)),
        compiler_params=pltpu.CompilerParams(vmem_limit_bytes=VMEM // 2),
        name="layer",
    )(parity, inputs, mean, inputs, inputs, bias, cotangent, traded, traded)


def body(features, neigh_weight, self_weight, bias, neighbors, boundary, counts, cotangent):
    columns, nodes = features.shape
    partitions = lax.axis_size("vertex")
    shares = lax.axis_size("feat")
    seed_count = neighbors.shape[1]
    hidden = cotangent.shape[0]
    pair = 2 * hidden
    odd = lax.axis_index("feat") % 2
    parity = odd.astype(jnp.int32).reshape(1)
    bias = bias.reshape(1, hidden)
    trade = [(f, f ^ 1) for f in range(shares)]

    place = lax.axis_index("vertex").astype(jnp.int32).reshape(1)
    near = list(pick(place, features, boundary[0], counts))
    near[1:], late = lax.optimization_barrier((near[1:], parity))
    for k in range(1, RADIX):
        near[k] = lax.ppermute(
            near[k], "vertex", [(v, v // RADIX * RADIX + (v + k) % RADIX) for v in range(partitions)])
    inputs, traded = pack(late, features, neigh_weight, self_weight, cotangent, bias, shares)
    near[1:], inputs = lax.optimization_barrier((near[1:], inputs))
    inputs = lax.all_to_all(inputs, "feat", split_axis=0, concat_axis=0, tiled=True)
    far = list(regroup(near))
    far, early, traded = lax.optimization_barrier((far, neighbors, traded))
    for j in range(1, RADIX):
        far[j - 1] = lax.ppermute(
            far[j - 1], "vertex", [(v, (v + j * RADIX) % partitions) for v in range(partitions)])
    traded = lax.ppermute(traded, "feat", trade)
    remote, local, rank, low = first_tables(early, features, FIRST)
    mean = neighbor_mean(place, remote, near, far, local, rank, low, neighbors, features, shares)
    mean, inputs, traded, parity = lax.optimization_barrier((mean, inputs, traded, parity))
    inputs = inputs.reshape(shares * columns, inputs.shape[2])
    mean = lax.all_to_all(mean, "feat", split_axis=0, concat_axis=0, tiled=True)
    mean = mean.reshape(shares * columns, mean.shape[2])
    kept, sent, grad = layer(parity, inputs, mean, bias, cotangent, traded, shares)
    members = [[v * shares + 2 * q + k for v in range(partitions) for k in range(2)] for q in range(shares // 2)]
    grad = lax.all_to_all(
        grad, ("vertex", "feat"), split_axis=0, concat_axis=0, tiled=True, axis_index_groups=members)
    other = lax.ppermute(sent, "feat", trade)
    activation = jnp.concatenate(
        [jnp.where(odd == 1, other, kept), jnp.where(odd == 1, kept, other)], axis=1)

    factor = 1.0 / math.sqrt(seed_count * partitions)
    grad = jnp.sum(grad.astype(jnp.float32), axis=0) * factor
    bias_out = grad[columns, :hidden] + grad[columns + 1, :hidden]
    swap = [(v * shares + f, f * shares + v) for v in range(partitions) for f in range(shares)]
    grad = lax.ppermute(grad[:columns], ("vertex", "feat"), swap)
    return activation, grad[:, :hidden], grad[:, hidden:], bias_out


def solution(mesh):
    placed = (
        P("feat", "vertex"),
        P("feat", None),
        P("feat", None),
        P("feat"),
        P(None, "vertex"),
        P("vertex", None, None),
        P("vertex", None),
        P("feat", "vertex"),
    )
    return jax.shard_map(
        body,
        mesh=mesh,
        in_specs=placed,
        out_specs=(P("feat", "vertex"), P("feat", "vertex"), P("feat", "vertex"), P("feat")),
        check_vma=False,
    )
```

```python
import functools
import math

import jax
import jax.numpy as jnp
from jax import lax
from jax.experimental import pallas as pl
from jax.experimental.pallas import tpu as pltpu
from jax.sharding import PartitionSpec as P

LOW = 256
ONES = jnp.float8_e4m3fn
UNROLL = 8
FIRST = 4
RADIX = 4
PAD = 32
GROUP = 8
SUMS = 8
EXTRA = 16
VMEM = 60 * 1024 * 1024
NT = (((1,), (1,)), ((), ()))
TN = (((0,), (0,)), ((), ()))


def one_hot(keys, rows):
    width = keys.shape[1]
    wide = jnp.broadcast_to(keys, (16, width)).astype(jnp.bfloat16)
    base = lax.broadcasted_iota(jnp.int32, (rows, width), 0).astype(jnp.float32).astype(jnp.bfloat16)
    base = base.reshape(rows // 16, 16, width)
    hit = base == wide[None]
    return jnp.where(hit, jnp.bfloat16(1), jnp.bfloat16(0)).reshape(rows, width)


def relative(place, j, k):
    return ((place // RADIX + j) % RADIX) * RADIX + (place % RADIX + k) % RADIX


def pick_kernel(place_ref, features_ref, boundary_ref, counts_ref, *refs):
    out_refs, rows_ref = refs[:RADIX], refs[RADIX]
    columns, nodes = features_ref.shape
    groups = nodes // LOW
    capacity = boundary_ref.shape[1]
    for high in range(groups):
        rows_ref[pl.ds(high * columns, columns), :] = features_ref[:, pl.ds(high * LOW, LOW)]
    slot = lax.broadcasted_iota(jnp.int32, (1, capacity), 1)
    for k in range(RADIX):
        for j in range(RADIX):
            p = relative(place_ref[0], j, k)
            listed = boundary_ref[pl.ds(p, 1), :]
            used = slot < counts_ref[0, p]
            high = jnp.where(used, listed >> 8, -1)
            low = (listed & (LOW - 1)).astype(jnp.float32)
            found = jnp.dot(rows_ref[...], one_hot(low, LOW), preferred_element_type=jnp.float32)
            total = jnp.zeros((columns, capacity), jnp.float32)
            for group in range(groups):
                total = total + jnp.where(high == group, found[group * columns:(group + 1) * columns], 0.0)
            out_refs[k][j] = total.astype(jnp.bfloat16)


def pick(place, features, boundary, counts):
    columns, nodes = features.shape
    capacity = boundary.shape[1]
    vm = pl.BlockSpec(memory_space=pltpu.VMEM)
    sm = pl.BlockSpec(memory_space=pltpu.SMEM)
    return pl.pallas_call(
        pick_kernel,
        out_shape=(jax.ShapeDtypeStruct((RADIX, columns, capacity), jnp.bfloat16),) * RADIX,
        in_specs=[sm, vm, vm, sm],
        out_specs=(vm,) * RADIX,
        scratch_shapes=[pltpu.VMEM((columns * nodes // LOW, LOW), jnp.bfloat16)],
        compiler_params=pltpu.CompilerParams(vmem_limit_bytes=VMEM),
        name="pick",
    )(place, features, boundary, counts)


def regroup_kernel(*refs):
    in_refs, out_refs = refs[:RADIX], refs[RADIX:]
    for j, out_ref in enumerate(out_refs, 1):
        for k, in_ref in enumerate(in_refs):
            out_ref[k] = in_ref[j]


def regroup(pieces):
    vm = pl.BlockSpec(memory_space=pltpu.VMEM)
    return pl.pallas_call(
        regroup_kernel,
        out_shape=(jax.ShapeDtypeStruct(pieces[0].shape, jnp.bfloat16),) * (RADIX - 1),
        in_specs=[vm] * RADIX,
        out_specs=(vm,) * (RADIX - 1),
        name="regroup",
    )(*pieces)


def pack_kernel(parity_ref, features_ref, neigh_weight_ref, self_weight_ref, cotangent_ref, bias_ref,
                inputs_ref, traded_ref):
    shares, _, width = inputs_ref.shape
    half = features_ref.shape[1] // 2
    wide = (width - half) // 2
    for share in range(shares):
        inputs_ref[share, :, pl.ds(0, half)] = features_ref[:, pl.ds((share % 2) * half, half)]
        at = pl.ds((share // 2) * wide, wide)
        inputs_ref[share, :, pl.ds(half, wide)] = neigh_weight_ref[:, at]
        inputs_ref[share, :, pl.ds(half + wide, wide)] = self_weight_ref[:, at]
    hidden = cotangent_ref.shape[0]
    traded_ref[pl.ds(0, hidden), :] = cotangent_ref[
        :, pl.ds(pl.multiple_of((1 - parity_ref[0]) * half, half), half)]
    bias = jnp.concatenate([bias_ref[...], jnp.zeros((1, half - hidden), jnp.bfloat16)], axis=1)
    traded_ref[pl.ds(hidden, EXTRA), :] = jnp.broadcast_to(bias.astype(jnp.float32), (EXTRA, half)).astype(jnp.bfloat16)


def pack(parity, features, neigh_weight, self_weight, cotangent, bias, shares):
    columns = features.shape[0]
    hidden, seed_count = cotangent.shape
    half = seed_count // 2
    whole = lambda i: (0, 0)
    return pl.pallas_call(
        pack_kernel,
        grid=(1,),
        out_shape=(jax.ShapeDtypeStruct((shares, columns, half + 4 * hidden), jnp.bfloat16),
                   jax.ShapeDtypeStruct((hidden + EXTRA, half), jnp.bfloat16)),
        in_specs=[pl.BlockSpec(memory_space=pltpu.SMEM),
                  pl.BlockSpec((columns, seed_count), whole),
                  pl.BlockSpec(neigh_weight.shape, whole),
                  pl.BlockSpec(self_weight.shape, whole),
                  pl.BlockSpec(cotangent.shape, whole),
                  pl.BlockSpec(bias.shape, whole)],
        out_specs=(pl.BlockSpec((shares, columns, half + 4 * hidden), lambda i: (0, 0, 0)),
                   pl.BlockSpec((hidden + EXTRA, half), whole)),
        compiler_params=pltpu.CompilerParams(vmem_limit_bytes=VMEM),
        name="pack",
    )(parity, features, neigh_weight, self_weight, cotangent, bias)


def fill_table(first_group, groups, rank_ref, low_ref, store):
    def pairs(i, carry):
        for unrolled in range(UNROLL):
            pair = i * UNROLL + unrolled
            found = []
            for k in range(2):
                group = first_group + 2 * pair + k
                left = one_hot(rank_ref[pl.ds(group, 1), :], rank_ref.shape[1]).astype(ONES)
                right = one_hot(low_ref[pl.ds(group, 1), :], LOW).astype(ONES)
                table = lax.dot_general(left, right, NT, preferred_element_type=jnp.float32)
                found.append(table.reshape(table.shape[0] // GROUP, GROUP, LOW))
            rows = pl.ds(pl.multiple_of(pair * 2 * GROUP, 2 * GROUP), 2 * GROUP)
            store(rows, jnp.concatenate(found, axis=1).astype(jnp.bfloat16))
        return carry

    lax.fori_loop(0, groups // 2 // UNROLL, pairs, 0)


def table_kernel(neighbors_ref, features_ref, remote_ref, local_ref, rank_ref, low_ref, local_table_ref):
    slot_count, seed_count = neighbors_ref.shape
    group_count = seed_count // GROUP
    rows, half = local_table_ref.shape
    highs = half // LOW
    step = pl.program_id(0)

    @pl.when(step == 0)
    def _():
        values = []
        for member in range(GROUP):
            value = neighbors_ref[:, pl.ds(member * group_count, group_count)].astype(jnp.float32)
            values.append(jnp.concatenate(
                [value, jnp.full((PAD - slot_count, group_count), -1.0, jnp.float32)], axis=0))
        value = jnp.concatenate(values, axis=0).T
        member = lax.broadcasted_iota(jnp.int32, value.shape, 1) // PAD
        high = jnp.floor(value * (1.0 / LOW))
        rank_ref[...] = jnp.where(value < 0, -1.0, high * GROUP + member.astype(jnp.float32))
        low_ref[...] = value - high * LOW

    def store(at, table):
        for high in range(highs):
            local_table_ref[at, pl.ds(high * LOW, LOW)] = table[high]
            remote_ref[at, pl.ds(high * LOW, LOW)] = table[highs + high]

    groups = rows // GROUP
    fill_table(step * groups, groups, rank_ref, low_ref, store)
    local_ref[...] = lax.dot_general(
        local_table_ref[...], features_ref[...], NT, preferred_element_type=jnp.float32)


def first_tables(neighbors, features, blocks, rows=256):
    slot_count, seed_count = neighbors.shape
    columns, nodes = features.shape
    group_count = seed_count // GROUP
    keys = jax.ShapeDtypeStruct((group_count, GROUP * PAD), jnp.float32)
    whole = lambda i: (0, 0)
    return pl.pallas_call(
        table_kernel,
        grid=(blocks,),
        out_shape=(jax.ShapeDtypeStruct((blocks * rows, nodes), jnp.bfloat16),
                   jax.ShapeDtypeStruct((blocks * rows, columns), jnp.float32), keys, keys),
        in_specs=[pl.BlockSpec((slot_count, seed_count), whole), pl.BlockSpec((columns, nodes), whole)],
        out_specs=(pl.BlockSpec((rows, nodes), lambda i: (i, 0)),
                   pl.BlockSpec((rows, columns), lambda i: (i, 0)),
                   pl.BlockSpec(keys.shape, whole), pl.BlockSpec(keys.shape, whole)),
        scratch_shapes=[pltpu.VMEM((rows, nodes), jnp.bfloat16)],
        compiler_params=pltpu.CompilerParams(vmem_limit_bytes=VMEM),
        name="first_tables",
    )(neighbors, features)


def mean_kernel(rows, place_ref, remote_ref, near_refs, far_refs, local_ref, rank_ref, low_ref, neighbors_ref,
                features_ref, out_ref, lookup_ref, sum_ref, table_ref, held_ref, sems):
    _, columns, capacity = near_refs[0].shape
    nodes = features_ref.shape[1]
    seed_count = sum_ref.shape[0]
    group_count = seed_count // GROUP
    blocks = held_ref.shape[0]
    copies = [
        pltpu.make_async_copy(remote_ref.at[pl.ds(k * rows, rows), :], held_ref.at[k], sems.at[k])
        for k in range(blocks)]
    for copy in copies:
        copy.start()
    lookup_ref[:, pl.ds(0, nodes)] = features_ref[...]
    for j in range(RADIX):
        for k in range(RADIX):
            source = relative(place_ref[0], RADIX - j, RADIX - k)
            at = pl.ds(pl.multiple_of(nodes + source * capacity, capacity), capacity)
            lookup_ref[:, at] = near_refs[k][0] if j == 0 else far_refs[j - 1][k]

    def store(at, table):
        for high in range(table.shape[0]):
            table_ref[at, pl.ds(high * LOW, LOW)] = table[high]

    def build(k, carry):
        fill_table(k * (rows // GROUP), rows // GROUP, rank_ref, low_ref, store)
        sum_ref[pl.ds(pl.multiple_of(k * rows, rows), rows), pl.ds(0, columns)] = lax.dot_general(
            table_ref[...], lookup_ref[...], NT, preferred_element_type=jnp.float32)
        return carry

    lax.fori_loop(blocks, seed_count // rows, build, 0)
    for k in range(blocks):
        copies[k].wait()
        at = pl.ds(k * rows, rows)
        sum_ref[at, pl.ds(0, columns)] = local_ref[at, :] + lax.dot_general(
            held_ref[k], lookup_ref[:, nodes:], NT, preferred_element_type=jnp.float32)

    degree = jnp.sum(jnp.where(neighbors_ref[...] >= 0, 1.0, 0.0), axis=0, keepdims=True)
    shares, _, half = out_ref.shape
    for member in range(GROUP):
        mine = sum_ref[pl.ds(member, group_count, stride=GROUP), :].T[:columns]
        start = member * group_count
        mine = mine / degree[:, start:start + group_count]
        mine = mine.astype(jnp.bfloat16)
        for share in range(start // half, shares, 2):
            out_ref[share, :, pl.ds(start % half, group_count)] = mine


def neighbor_mean(place, remote, near, far, local, rank, low, neighbors, features, shares, rows=256):
    slot_count, seed_count = neighbors.shape
    columns, nodes = features.shape
    capacity = near[0].shape[2]
    blocks = remote.shape[0] // rows
    lookup_width = nodes + RADIX * RADIX * capacity
    vm = pl.BlockSpec(memory_space=pltpu.VMEM)

    def kernel(place_ref, remote_ref, *refs):
        mean_kernel(rows, place_ref, remote_ref, refs[:RADIX], refs[RADIX:2 * RADIX - 1], *refs[2 * RADIX - 1:])

    return pl.pallas_call(
        kernel,
        out_shape=jax.ShapeDtypeStruct((shares, columns, seed_count // 2), jnp.bfloat16),
        in_specs=[pl.BlockSpec(memory_space=pltpu.SMEM), pl.BlockSpec(memory_space=pl.ANY)]
        + [vm] * (2 * RADIX - 1 + 5),
        out_specs=vm,
        scratch_shapes=[pltpu.VMEM((columns, lookup_width), jnp.bfloat16),
                        pltpu.VMEM((seed_count, 128), jnp.float32),
                        pltpu.VMEM((rows, lookup_width), jnp.bfloat16),
                        pltpu.VMEM((blocks, rows, nodes), jnp.bfloat16),
                        pltpu.SemaphoreType.DMA((blocks,))],
        compiler_params=pltpu.CompilerParams(vmem_limit_bytes=VMEM),
        name="mean",
    )(place, remote, *near, *far, local, rank, low, neighbors, features)


def layer_kernel(parity_ref, own_ref, mean_ref, neigh_weight_ref, self_weight_ref, bias_ref, cotangent_ref,
                 traded_ref, traded_bias_ref, kept_ref, sent_ref, grad_ref, total_ref, sums_ref):
    step = pl.program_id(0)
    odd = parity_ref[0] == 1
    hidden = cotangent_ref.shape[0]

    @pl.when(step == 0)
    def _():
        total_ref[...] = jnp.zeros_like(total_ref)
        sums_ref[...] = jnp.zeros_like(sums_ref)

    def ordered(mine, other):
        return jnp.concatenate([jnp.where(odd, other, mine), jnp.where(odd, mine, other)], axis=0)

    mine = bias_ref[...].astype(jnp.float32)
    theirs = traded_bias_ref[:1, :hidden].astype(jnp.float32)
    bias = jnp.concatenate([jnp.where(odd, theirs, mine), jnp.where(odd, mine, theirs)], axis=1)
    row = lax.broadcasted_iota(jnp.int32, (EXTRA, 2 * hidden), 0)
    bias = jnp.where(row == 0, bias, 0.0).astype(jnp.bfloat16)
    ones = jnp.ones((EXTRA, own_ref.shape[1]), jnp.bfloat16)
    cotangent = ordered(cotangent_ref[...].astype(jnp.float32), traded_ref[...].astype(jnp.float32))
    preact = (
        lax.dot_general(neigh_weight_ref[...], mean_ref[...], TN, preferred_element_type=jnp.float32)
        + lax.dot_general(self_weight_ref[...], own_ref[...], TN, preferred_element_type=jnp.float32)
        + lax.dot_general(bias, ones, TN, preferred_element_type=jnp.float32)
    )
    decay = jnp.exp(jnp.minimum(preact, 0.0))
    activation = jnp.where(preact > 0, preact, decay - 1.0)
    kept_ref[...] = jnp.where(odd, activation[hidden:], activation[:hidden]).astype(jnp.bfloat16)
    sent_ref[...] = jnp.where(odd, activation[:hidden], activation[hidden:]).astype(jnp.bfloat16)
    slope = jnp.where(preact > 0, 1.0, decay)
    grad_pre = (cotangent * slope).astype(jnp.bfloat16)
    first, second = grad_pre[:hidden], grad_pre[hidden:]
    blank = jnp.zeros_like(first)
    for_neigh = jnp.concatenate([first, blank, second, blank], axis=0)
    for_own = jnp.concatenate([blank, first, blank, second], axis=0)
    total_ref[...] += (
        lax.dot_general(mean_ref[...], for_neigh, NT, preferred_element_type=jnp.float32)
        + lax.dot_general(own_ref[...], for_own, NT, preferred_element_type=jnp.float32))
    sums_ref[...] += lax.dot_general(ones[:SUMS], for_neigh, NT, preferred_element_type=jnp.float32)

    @pl.when(step == pl.num_programs(0) - 1)
    def _():
        chunks, rows, width = grad_ref.shape
        columns = rows - SUMS
        sums = sums_ref[...]
        high = sums.astype(jnp.bfloat16).astype(jnp.float32)
        row = lax.broadcasted_iota(jnp.int32, sums.shape, 0)
        extra = jnp.where(row == 0, high, jnp.where(row == 1, sums - high, 0.0))
        for chunk in range(chunks):
            at = slice((chunk % 2) * width, (chunk % 2 + 1) * width)
            mine = total_ref[pl.ds((chunk // 2) * columns, columns), at]
            grad_ref[chunk] = jnp.concatenate([mine, extra[:, at]], axis=0).astype(jnp.bfloat16)


def layer(parity, inputs, mean, bias, cotangent, traded, shares, block=512):
    features, half = mean.shape
    hidden = cotangent.shape[0]
    pair = 2 * hidden
    blocks = half // block
    whole = lambda i, parity: (0, 0)
    part = lambda i, parity: (0, i)
    grads = (2 * shares, features // shares + SUMS, pair)
    return pl.pallas_call(
        layer_kernel,
        grid_spec=pltpu.PrefetchScalarGridSpec(
            num_scalar_prefetch=1,
            grid=(blocks,),
            in_specs=[pl.BlockSpec((features, block), part),
                      pl.BlockSpec((features, block), part),
                      pl.BlockSpec((features, pair), lambda i, parity: (0, half // pair)),
                      pl.BlockSpec((features, pair), lambda i, parity: (0, half // pair + 1)),
                      pl.BlockSpec((1, hidden), whole),
                      pl.BlockSpec((hidden, block), lambda i, parity: (0, i + parity[0] * blocks)),
                      pl.BlockSpec((hidden, block), part),
                      pl.BlockSpec((EXTRA, 128), lambda i, parity: (hidden // EXTRA, 0))],
            out_specs=(pl.BlockSpec((hidden, block), part),
                       pl.BlockSpec((hidden, block), part),
                       pl.BlockSpec(grads, lambda i, parity: (0, 0, 0))),
            scratch_shapes=[pltpu.VMEM((features, 2 * pair), jnp.float32),
                            pltpu.VMEM((SUMS, 2 * pair), jnp.float32)]),
        out_shape=(jax.ShapeDtypeStruct((hidden, half), jnp.bfloat16),
                   jax.ShapeDtypeStruct((hidden, half), jnp.bfloat16),
                   jax.ShapeDtypeStruct(grads, jnp.bfloat16)),
        compiler_params=pltpu.CompilerParams(vmem_limit_bytes=VMEM // 2),
        name="layer",
    )(parity, inputs, mean, inputs, inputs, bias, cotangent, traded, traded)


def body(features, neigh_weight, self_weight, bias, neighbors, boundary, counts, cotangent):
    columns, nodes = features.shape
    partitions = lax.axis_size("vertex")
    shares = lax.axis_size("feat")
    seed_count = neighbors.shape[1]
    hidden = cotangent.shape[0]
    pair = 2 * hidden
    odd = lax.axis_index("feat") % 2
    parity = odd.astype(jnp.int32).reshape(1)
    bias = bias.reshape(1, hidden)
    trade = [(f, f ^ 1) for f in range(shares)]

    place = lax.axis_index("vertex").astype(jnp.int32).reshape(1)
    near = list(pick(place, features, boundary[0], counts))
    near[1:], late = lax.optimization_barrier((near[1:], parity))
    for k in range(1, RADIX):
        near[k] = lax.ppermute(
            near[k], "vertex", [(v, v // RADIX * RADIX + (v + k) % RADIX) for v in range(partitions)])
    inputs, traded = pack(late, features, neigh_weight, self_weight, cotangent, bias, shares)
    near[1:], inputs = lax.optimization_barrier((near[1:], inputs))
    far = list(regroup(near))
    far, early, traded, inputs = lax.optimization_barrier((far, neighbors, traded, inputs))
    inputs = lax.all_to_all(inputs, "feat", split_axis=0, concat_axis=0, tiled=True)
    for j in range(1, RADIX):
        far[j - 1] = lax.ppermute(
            far[j - 1], "vertex", [(v, (v + j * RADIX) % partitions) for v in range(partitions)])
    traded = lax.ppermute(traded, "feat", trade)
    remote, local, rank, low = first_tables(early, features, FIRST)
    mean = neighbor_mean(place, remote, near, far, local, rank, low, neighbors, features, shares)
    mean, inputs, traded, parity = lax.optimization_barrier((mean, inputs, traded, parity))
    inputs = inputs.reshape(shares * columns, inputs.shape[2])
    mean = lax.all_to_all(mean, "feat", split_axis=0, concat_axis=0, tiled=True)
    mean = mean.reshape(shares * columns, mean.shape[2])
    kept, sent, grad = layer(parity, inputs, mean, bias, cotangent, traded, shares)
    members = [[v * shares + 2 * q + k for v in range(partitions) for k in range(2)] for q in range(shares // 2)]
    grad = lax.all_to_all(
        grad, ("vertex", "feat"), split_axis=0, concat_axis=0, tiled=True, axis_index_groups=members)
    other = lax.ppermute(sent, "feat", trade)
    activation = jnp.concatenate(
        [jnp.where(odd == 1, other, kept), jnp.where(odd == 1, kept, other)], axis=1)

    factor = 1.0 / math.sqrt(seed_count * partitions)
    grad = jnp.sum(grad.astype(jnp.float32), axis=0) * factor
    bias_out = grad[columns, :hidden] + grad[columns + 1, :hidden]
    swap = [(v * shares + f, f * shares + v) for v in range(partitions) for f in range(shares)]
    grad = lax.ppermute(grad[:columns], ("vertex", "feat"), swap)
    return activation, grad[:, :hidden], grad[:, hidden:], bias_out


def solution(mesh):
    placed = (
        P("feat", "vertex"),
        P("feat", None),
        P("feat", None),
        P("feat"),
        P(None, "vertex"),
        P("vertex", None, None),
        P("vertex", None),
        P("feat", "vertex"),
    )
    return jax.shard_map(
        body,
        mesh=mesh,
        in_specs=placed,
        out_specs=(P("feat", "vertex"), P("feat", "vertex"), P("feat", "vertex"), P("feat")),
        check_vma=False,
    )
```

```python
import functools
import math

import jax
import jax.numpy as jnp
from jax import lax
from jax.experimental import pallas as pl
from jax.experimental.pallas import tpu as pltpu
from jax.sharding import PartitionSpec as P

LOW = 256
ONES = jnp.float8_e4m3fn
UNROLL = 16
FIRST = 4
RADIX = 4
PAD = 32
GROUP = 8
SUMS = 8
EXTRA = 16
VMEM = 60 * 1024 * 1024
NT = (((1,), (1,)), ((), ()))
TN = (((0,), (0,)), ((), ()))


def one_hot(keys, rows):
    width = keys.shape[1]
    wide = jnp.broadcast_to(keys, (16, width)).astype(jnp.bfloat16)
    base = lax.broadcasted_iota(jnp.int32, (rows, width), 0).astype(jnp.float32).astype(jnp.bfloat16)
    base = base.reshape(rows // 16, 16, width)
    hit = base == wide[None]
    return jnp.where(hit, jnp.bfloat16(1), jnp.bfloat16(0)).reshape(rows, width)


def relative(place, j, k):
    return ((place // RADIX + j) % RADIX) * RADIX + (place % RADIX + k) % RADIX


def one_hot_small(keys, ones, rows):
    width = keys.shape[1]
    wide = jnp.broadcast_to(keys - 128.0, (32, width)).astype(jnp.int32).astype(jnp.int8)
    ones = jnp.broadcast_to(ones, (32, width)).astype(ONES)
    base = (lax.broadcasted_iota(jnp.int32, (rows, width), 0) - 128).astype(jnp.int8)
    hit = base.reshape(rows // 32, 32, width) == wide[None]
    return jnp.where(hit, ones[None], jnp.zeros((), ONES)).reshape(rows, width)


def pick_kernel(place_ref, features_ref, boundary_ref, counts_ref, *refs):
    out_refs, rows_ref = refs[:RADIX], refs[RADIX]
    columns, nodes = features_ref.shape
    groups = nodes // LOW
    capacity = boundary_ref.shape[1]
    for high in range(groups):
        rows_ref[pl.ds(high * columns, columns), :] = features_ref[:, pl.ds(high * LOW, LOW)]
    slot = lax.broadcasted_iota(jnp.int32, (1, capacity), 1)
    for k in range(RADIX):
        for j in range(RADIX):
            p = relative(place_ref[0], j, k)
            listed = boundary_ref[pl.ds(p, 1), :]
            used = slot < counts_ref[0, p]
            high = jnp.where(used, listed >> 8, -1)
            low = (listed & (LOW - 1)).astype(jnp.float32)
            found = jnp.dot(rows_ref[...], one_hot(low, LOW), preferred_element_type=jnp.float32)
            total = jnp.zeros((columns, capacity), jnp.float32)
            for group in range(groups):
                total = total + jnp.where(high == group, found[group * columns:(group + 1) * columns], 0.0)
            out_refs[k][j] = total.astype(jnp.bfloat16)


def pick(place, features, boundary, counts):
    columns, nodes = features.shape
    capacity = boundary.shape[1]
    vm = pl.BlockSpec(memory_space=pltpu.VMEM)
    sm = pl.BlockSpec(memory_space=pltpu.SMEM)
    return pl.pallas_call(
        pick_kernel,
        out_shape=(jax.ShapeDtypeStruct((RADIX, columns, capacity), jnp.bfloat16),) * RADIX,
        in_specs=[sm, vm, vm, sm],
        out_specs=(vm,) * RADIX,
        scratch_shapes=[pltpu.VMEM((columns * nodes // LOW, LOW), jnp.bfloat16)],
        compiler_params=pltpu.CompilerParams(vmem_limit_bytes=VMEM),
        name="pick",
    )(place, features, boundary, counts)


def regroup_kernel(*refs):
    in_refs, out_refs = refs[:RADIX], refs[RADIX:]
    for j, out_ref in enumerate(out_refs, 1):
        for k, in_ref in enumerate(in_refs):
            out_ref[k] = in_ref[j]


def regroup(pieces):
    vm = pl.BlockSpec(memory_space=pltpu.VMEM)
    return pl.pallas_call(
        regroup_kernel,
        out_shape=(jax.ShapeDtypeStruct(pieces[0].shape, jnp.bfloat16),) * (RADIX - 1),
        in_specs=[vm] * RADIX,
        out_specs=(vm,) * (RADIX - 1),
        name="regroup",
    )(*pieces)


def pack_kernel(parity_ref, features_ref, neigh_weight_ref, self_weight_ref, cotangent_ref, bias_ref,
                inputs_ref, traded_ref):
    shares, _, width = inputs_ref.shape
    half = features_ref.shape[1] // 2
    wide = (width - half) // 2
    for share in range(shares):
        inputs_ref[share, :, pl.ds(0, half)] = features_ref[:, pl.ds((share % 2) * half, half)]
        at = pl.ds((share // 2) * wide, wide)
        inputs_ref[share, :, pl.ds(half, wide)] = neigh_weight_ref[:, at]
        inputs_ref[share, :, pl.ds(half + wide, wide)] = self_weight_ref[:, at]
    hidden = cotangent_ref.shape[0]
    traded_ref[pl.ds(0, hidden), :] = cotangent_ref[
        :, pl.ds(pl.multiple_of((1 - parity_ref[0]) * half, half), half)]
    bias = jnp.concatenate([bias_ref[...], jnp.zeros((1, half - hidden), jnp.bfloat16)], axis=1)
    traded_ref[pl.ds(hidden, EXTRA), :] = jnp.broadcast_to(bias.astype(jnp.float32), (EXTRA, half)).astype(jnp.bfloat16)


def pack(parity, features, neigh_weight, self_weight, cotangent, bias, shares):
    columns = features.shape[0]
    hidden, seed_count = cotangent.shape
    half = seed_count // 2
    whole = lambda i: (0, 0)
    return pl.pallas_call(
        pack_kernel,
        grid=(1,),
        out_shape=(jax.ShapeDtypeStruct((shares, columns, half + 4 * hidden), jnp.bfloat16),
                   jax.ShapeDtypeStruct((hidden + EXTRA, half), jnp.bfloat16)),
        in_specs=[pl.BlockSpec(memory_space=pltpu.SMEM),
                  pl.BlockSpec((columns, seed_count), whole),
                  pl.BlockSpec(neigh_weight.shape, whole),
                  pl.BlockSpec(self_weight.shape, whole),
                  pl.BlockSpec(cotangent.shape, whole),
                  pl.BlockSpec(bias.shape, whole)],
        out_specs=(pl.BlockSpec((shares, columns, half + 4 * hidden), lambda i: (0, 0, 0)),
                   pl.BlockSpec((hidden + EXTRA, half), whole)),
        compiler_params=pltpu.CompilerParams(vmem_limit_bytes=VMEM),
        name="pack",
    )(parity, features, neigh_weight, self_weight, cotangent, bias)


def fill_table(first_group, groups, rank_ref, low_ref, store):
    def pairs(i, carry):
        for unrolled in range(UNROLL):
            pair = i * UNROLL + unrolled
            found = []
            for k in range(2):
                group = first_group + 2 * pair + k
                rank = rank_ref[pl.ds(group, 1), :]
                named = jnp.where(rank < 0, 0.0, 1.0)
                left = one_hot_small(jnp.maximum(rank, 0.0), named, rank.shape[1])
                right = one_hot_small(low_ref[pl.ds(group, 1), :], named, LOW)
                table = lax.dot_general(left, right, NT, preferred_element_type=jnp.float32)
                found.append(table.reshape(table.shape[0] // GROUP, GROUP, LOW))
            rows = pl.ds(pl.multiple_of(pair * 2 * GROUP, 2 * GROUP), 2 * GROUP)
            store(rows, jnp.concatenate(found, axis=1).astype(jnp.bfloat16))
        return carry

    lax.fori_loop(0, groups // 2 // UNROLL, pairs, 0)


def table_kernel(neighbors_ref, features_ref, remote_ref, local_ref, rank_ref, low_ref, local_table_ref):
    slot_count, seed_count = neighbors_ref.shape
    group_count = seed_count // GROUP
    rows, half = local_table_ref.shape
    highs = half // LOW
    step = pl.program_id(0)

    @pl.when(step == 0)
    def _():
        values = []
        for member in range(GROUP):
            value = neighbors_ref[:, pl.ds(member * group_count, group_count)].astype(jnp.float32)
            values.append(jnp.concatenate(
                [value, jnp.full((PAD - slot_count, group_count), -1.0, jnp.float32)], axis=0))
        value = jnp.concatenate(values, axis=0).T
        member = lax.broadcasted_iota(jnp.int32, value.shape, 1) // PAD
        high = jnp.floor(value * (1.0 / LOW))
        rank_ref[...] = jnp.where(value < 0, -1.0, high * GROUP + member.astype(jnp.float32))
        low_ref[...] = value - high * LOW

    def store(at, table):
        for high in range(highs):
            local_table_ref[at, pl.ds(high * LOW, LOW)] = table[high]
            remote_ref[at, pl.ds(high * LOW, LOW)] = table[highs + high]

    groups = rows // GROUP
    fill_table(step * groups, groups, rank_ref, low_ref, store)
    local_ref[...] = lax.dot_general(
        local_table_ref[...], features_ref[...], NT, preferred_element_type=jnp.float32)


def first_tables(neighbors, features, blocks, rows=256):
    slot_count, seed_count = neighbors.shape
    columns, nodes = features.shape
    group_count = seed_count // GROUP
    keys = jax.ShapeDtypeStruct((group_count, GROUP * PAD), jnp.float32)
    whole = lambda i: (0, 0)
    return pl.pallas_call(
        table_kernel,
        grid=(blocks,),
        out_shape=(jax.ShapeDtypeStruct((blocks * rows, nodes), jnp.bfloat16),
                   jax.ShapeDtypeStruct((blocks * rows, columns), jnp.float32), keys, keys),
        in_specs=[pl.BlockSpec((slot_count, seed_count), whole), pl.BlockSpec((columns, nodes), whole)],
        out_specs=(pl.BlockSpec((rows, nodes), lambda i: (i, 0)),
                   pl.BlockSpec((rows, columns), lambda i: (i, 0)),
                   pl.BlockSpec(keys.shape, whole), pl.BlockSpec(keys.shape, whole)),
        scratch_shapes=[pltpu.VMEM((rows, nodes), jnp.bfloat16)],
        compiler_params=pltpu.CompilerParams(vmem_limit_bytes=VMEM),
        name="first_tables",
    )(neighbors, features)


def mean_kernel(rows, place_ref, remote_ref, near_refs, far_refs, local_ref, rank_ref, low_ref, neighbors_ref,
                features_ref, out_ref, lookup_ref, sum_ref, table_ref, held_ref, sems):
    _, columns, capacity = near_refs[0].shape
    nodes = features_ref.shape[1]
    seed_count = sum_ref.shape[0]
    group_count = seed_count // GROUP
    blocks = held_ref.shape[0]
    copies = [
        pltpu.make_async_copy(remote_ref.at[pl.ds(k * rows, rows), :], held_ref.at[k], sems.at[k])
        for k in range(blocks)]
    for copy in copies:
        copy.start()
    lookup_ref[:, pl.ds(0, nodes)] = features_ref[...]
    for j in range(RADIX):
        for k in range(RADIX):
            source = relative(place_ref[0], RADIX - j, RADIX - k)
            at = pl.ds(pl.multiple_of(nodes + source * capacity, capacity), capacity)
            lookup_ref[:, at] = near_refs[k][0] if j == 0 else far_refs[j - 1][k]

    def store(at, table):
        for high in range(table.shape[0]):
            table_ref[at, pl.ds(high * LOW, LOW)] = table[high]

    def build(k, carry):
        fill_table(k * (rows // GROUP), rows // GROUP, rank_ref, low_ref, store)
        sum_ref[pl.ds(pl.multiple_of(k * rows, rows), rows), pl.ds(0, columns)] = lax.dot_general(
            table_ref[...], lookup_ref[...], NT, preferred_element_type=jnp.float32)
        return carry

    lax.fori_loop(blocks, seed_count // rows, build, 0)
    for k in range(blocks):
        copies[k].wait()
        at = pl.ds(k * rows, rows)
        sum_ref[at, pl.ds(0, columns)] = local_ref[at, :] + lax.dot_general(
            held_ref[k], lookup_ref[:, nodes:], NT, preferred_element_type=jnp.float32)

    degree = jnp.sum(jnp.where(neighbors_ref[...] >= 0, 1.0, 0.0), axis=0, keepdims=True)
    shares, _, half = out_ref.shape
    for member in range(GROUP):
        mine = sum_ref[pl.ds(member, group_count, stride=GROUP), :].T[:columns]
        start = member * group_count
        mine = mine / degree[:, start:start + group_count]
        mine = mine.astype(jnp.bfloat16)
        for share in range(start // half, shares, 2):
            out_ref[share, :, pl.ds(start % half, group_count)] = mine


def neighbor_mean(place, remote, near, far, local, rank, low, neighbors, features, shares, rows=256):
    slot_count, seed_count = neighbors.shape
    columns, nodes = features.shape
    capacity = near[0].shape[2]
    blocks = remote.shape[0] // rows
    lookup_width = nodes + RADIX * RADIX * capacity
    vm = pl.BlockSpec(memory_space=pltpu.VMEM)

    def kernel(place_ref, remote_ref, *refs):
        mean_kernel(rows, place_ref, remote_ref, refs[:RADIX], refs[RADIX:2 * RADIX - 1], *refs[2 * RADIX - 1:])

    return pl.pallas_call(
        kernel,
        out_shape=jax.ShapeDtypeStruct((shares, columns, seed_count // 2), jnp.bfloat16),
        in_specs=[pl.BlockSpec(memory_space=pltpu.SMEM), pl.BlockSpec(memory_space=pl.ANY)]
        + [vm] * (2 * RADIX - 1 + 5),
        out_specs=vm,
        scratch_shapes=[pltpu.VMEM((columns, lookup_width), jnp.bfloat16),
                        pltpu.VMEM((seed_count, 128), jnp.float32),
                        pltpu.VMEM((rows, lookup_width), jnp.bfloat16),
                        pltpu.VMEM((blocks, rows, nodes), jnp.bfloat16),
                        pltpu.SemaphoreType.DMA((blocks,))],
        compiler_params=pltpu.CompilerParams(vmem_limit_bytes=VMEM),
        name="mean",
    )(place, remote, *near, *far, local, rank, low, neighbors, features)


def layer_kernel(parity_ref, own_ref, mean_ref, neigh_weight_ref, self_weight_ref, bias_ref, cotangent_ref,
                 traded_ref, traded_bias_ref, kept_ref, sent_ref, grad_ref, total_ref, sums_ref):
    step = pl.program_id(0)
    odd = parity_ref[0] == 1
    hidden = cotangent_ref.shape[0]

    @pl.when(step == 0)
    def _():
        total_ref[...] = jnp.zeros_like(total_ref)
        sums_ref[...] = jnp.zeros_like(sums_ref)

    def ordered(mine, other):
        return jnp.concatenate([jnp.where(odd, other, mine), jnp.where(odd, mine, other)], axis=0)

    mine = bias_ref[...].astype(jnp.float32)
    theirs = traded_bias_ref[:1, :hidden].astype(jnp.float32)
    bias = jnp.concatenate([jnp.where(odd, theirs, mine), jnp.where(odd, mine, theirs)], axis=1)
    row = lax.broadcasted_iota(jnp.int32, (EXTRA, 2 * hidden), 0)
    bias = jnp.where(row == 0, bias, 0.0).astype(jnp.bfloat16)
    ones = jnp.ones((EXTRA, own_ref.shape[1]), jnp.bfloat16)
    cotangent = ordered(cotangent_ref[...].astype(jnp.float32), traded_ref[...].astype(jnp.float32))
    preact = (
        lax.dot_general(neigh_weight_ref[...], mean_ref[...], TN, preferred_element_type=jnp.float32)
        + lax.dot_general(self_weight_ref[...], own_ref[...], TN, preferred_element_type=jnp.float32)
        + lax.dot_general(bias, ones, TN, preferred_element_type=jnp.float32)
    )
    decay = jnp.exp(jnp.minimum(preact, 0.0))
    activation = jnp.where(preact > 0, preact, decay - 1.0)
    kept_ref[...] = jnp.where(odd, activation[hidden:], activation[:hidden]).astype(jnp.bfloat16)
    sent_ref[...] = jnp.where(odd, activation[:hidden], activation[hidden:]).astype(jnp.bfloat16)
    slope = jnp.where(preact > 0, 1.0, decay)
    grad_pre = (cotangent * slope).astype(jnp.bfloat16)
    first, second = grad_pre[:hidden], grad_pre[hidden:]
    blank = jnp.zeros_like(first)
    for_neigh = jnp.concatenate([first, blank, second, blank], axis=0)
    for_own = jnp.concatenate([blank, first, blank, second], axis=0)
    total_ref[...] += (
        lax.dot_general(mean_ref[...], for_neigh, NT, preferred_element_type=jnp.float32)
        + lax.dot_general(own_ref[...], for_own, NT, preferred_element_type=jnp.float32))
    sums_ref[...] += lax.dot_general(ones[:SUMS], for_neigh, NT, preferred_element_type=jnp.float32)

    @pl.when(step == pl.num_programs(0) - 1)
    def _():
        chunks, rows, width = grad_ref.shape
        columns = rows - SUMS
        sums = sums_ref[...]
        high = sums.astype(jnp.bfloat16).astype(jnp.float32)
        row = lax.broadcasted_iota(jnp.int32, sums.shape, 0)
        extra = jnp.where(row == 0, high, jnp.where(row == 1, sums - high, 0.0))
        for chunk in range(chunks):
            at = slice((chunk % 2) * width, (chunk % 2 + 1) * width)
            mine = total_ref[pl.ds((chunk // 2) * columns, columns), at]
            grad_ref[chunk] = jnp.concatenate([mine, extra[:, at]], axis=0).astype(jnp.bfloat16)


def layer(parity, inputs, mean, bias, cotangent, traded, shares, block=512):
    features, half = mean.shape
    hidden = cotangent.shape[0]
    pair = 2 * hidden
    blocks = half // block
    whole = lambda i, parity: (0, 0)
    part = lambda i, parity: (0, i)
    grads = (2 * shares, features // shares + SUMS, pair)
    return pl.pallas_call(
        layer_kernel,
        grid_spec=pltpu.PrefetchScalarGridSpec(
            num_scalar_prefetch=1,
            grid=(blocks,),
            in_specs=[pl.BlockSpec((features, block), part),
                      pl.BlockSpec((features, block), part),
                      pl.BlockSpec((features, pair), lambda i, parity: (0, half // pair)),
                      pl.BlockSpec((features, pair), lambda i, parity: (0, half // pair + 1)),
                      pl.BlockSpec((1, hidden), whole),
                      pl.BlockSpec((hidden, block), lambda i, parity: (0, i + parity[0] * blocks)),
                      pl.BlockSpec((hidden, block), part),
                      pl.BlockSpec((EXTRA, 128), lambda i, parity: (hidden // EXTRA, 0))],
            out_specs=(pl.BlockSpec((hidden, block), part),
                       pl.BlockSpec((hidden, block), part),
                       pl.BlockSpec(grads, lambda i, parity: (0, 0, 0))),
            scratch_shapes=[pltpu.VMEM((features, 2 * pair), jnp.float32),
                            pltpu.VMEM((SUMS, 2 * pair), jnp.float32)]),
        out_shape=(jax.ShapeDtypeStruct((hidden, half), jnp.bfloat16),
                   jax.ShapeDtypeStruct((hidden, half), jnp.bfloat16),
                   jax.ShapeDtypeStruct(grads, jnp.bfloat16)),
        compiler_params=pltpu.CompilerParams(vmem_limit_bytes=VMEM // 2),
        name="layer",
    )(parity, inputs, mean, inputs, inputs, bias, cotangent, traded, traded)


def body(features, neigh_weight, self_weight, bias, neighbors, boundary, counts, cotangent):
    columns, nodes = features.shape
    partitions = lax.axis_size("vertex")
    shares = lax.axis_size("feat")
    seed_count = neighbors.shape[1]
    hidden = cotangent.shape[0]
    pair = 2 * hidden
    odd = lax.axis_index("feat") % 2
    parity = odd.astype(jnp.int32).reshape(1)
    bias = bias.reshape(1, hidden)
    trade = [(f, f ^ 1) for f in range(shares)]

    place = lax.axis_index("vertex").astype(jnp.int32).reshape(1)
    near = list(pick(place, features, boundary[0], counts))
    near[1:], late = lax.optimization_barrier((near[1:], parity))
    for k in range(1, RADIX):
        near[k] = lax.ppermute(
            near[k], "vertex", [(v, v // RADIX * RADIX + (v + k) % RADIX) for v in range(partitions)])
    inputs, traded = pack(late, features, neigh_weight, self_weight, cotangent, bias, shares)
    near[1:], inputs = lax.optimization_barrier((near[1:], inputs))
    far = list(regroup(near))
    far, early, traded, inputs = lax.optimization_barrier((far, neighbors, traded, inputs))
    inputs = lax.all_to_all(inputs, "feat", split_axis=0, concat_axis=0, tiled=True)
    for j in range(1, RADIX):
        far[j - 1] = lax.ppermute(
            far[j - 1], "vertex", [(v, (v + j * RADIX) % partitions) for v in range(partitions)])
    traded = lax.ppermute(traded, "feat", trade)
    remote, local, rank, low = first_tables(early, features, FIRST)
    mean = neighbor_mean(place, remote, near, far, local, rank, low, neighbors, features, shares)
    mean, inputs, traded, parity = lax.optimization_barrier((mean, inputs, traded, parity))
    inputs = inputs.reshape(shares * columns, inputs.shape[2])
    mean = lax.all_to_all(mean, "feat", split_axis=0, concat_axis=0, tiled=True)
    mean = mean.reshape(shares * columns, mean.shape[2])
    kept, sent, grad = layer(parity, inputs, mean, bias, cotangent, traded, shares)
    members = [[v * shares + 2 * q + k for v in range(partitions) for k in range(2)] for q in range(shares // 2)]
    grad = lax.all_to_all(
        grad, ("vertex", "feat"), split_axis=0, concat_axis=0, tiled=True, axis_index_groups=members)
    other = lax.ppermute(sent, "feat", trade)
    activation = jnp.concatenate(
        [jnp.where(odd == 1, other, kept), jnp.where(odd == 1, kept, other)], axis=1)

    factor = 1.0 / math.sqrt(seed_count * partitions)
    grad = jnp.sum(grad.astype(jnp.float32), axis=0) * factor
    bias_out = grad[columns, :hidden] + grad[columns + 1, :hidden]
    swap = [(v * shares + f, f * shares + v) for v in range(partitions) for f in range(shares)]
    grad = lax.ppermute(grad[:columns], ("vertex", "feat"), swap)
    return activation, grad[:, :hidden], grad[:, hidden:], bias_out


def solution(mesh):
    placed = (
        P("feat", "vertex"),
        P("feat", None),
        P("feat", None),
        P("feat"),
        P(None, "vertex"),
        P("vertex", None, None),
        P("vertex", None),
        P("feat", "vertex"),
    )
    return jax.shard_map(
        body,
        mesh=mesh,
        in_specs=placed,
        out_specs=(P("feat", "vertex"), P("feat", "vertex"), P("feat", "vertex"), P("feat")),
        check_vma=False,
    )
```

```python
import functools
import math

import jax
import jax.numpy as jnp
from jax import lax
from jax.experimental import pallas as pl
from jax.experimental.pallas import tpu as pltpu
from jax.sharding import PartitionSpec as P

LOW = 256
ONES = jnp.float8_e4m3fn
UNROLL = 16
FIRST = 5
RADIX = 4
PAD = 32
GROUP = 8
SUMS = 8
EXTRA = 16
VMEM = 60 * 1024 * 1024
NT = (((1,), (1,)), ((), ()))
TN = (((0,), (0,)), ((), ()))


def one_hot(keys, rows):
    width = keys.shape[1]
    wide = jnp.broadcast_to(keys, (16, width)).astype(jnp.bfloat16)
    base = lax.broadcasted_iota(jnp.int32, (rows, width), 0).astype(jnp.float32).astype(jnp.bfloat16)
    base = base.reshape(rows // 16, 16, width)
    hit = base == wide[None]
    return jnp.where(hit, jnp.bfloat16(1), jnp.bfloat16(0)).reshape(rows, width)


def relative(place, j, k):
    return ((place // RADIX + j) % RADIX) * RADIX + (place % RADIX + k) % RADIX


def one_hot_small(keys, ones, rows):
    width = keys.shape[1]
    wide = jnp.broadcast_to(keys - 128.0, (32, width)).astype(jnp.int32).astype(jnp.int8)
    ones = jnp.broadcast_to(ones, (32, width)).astype(ONES)
    base = (lax.broadcasted_iota(jnp.int32, (rows, width), 0) - 128).astype(jnp.int8)
    hit = base.reshape(rows // 32, 32, width) == wide[None]
    return jnp.where(hit, ones[None], jnp.zeros((), ONES)).reshape(rows, width)


def pick_kernel(place_ref, features_ref, boundary_ref, counts_ref, *refs):
    out_refs, rows_ref = refs[:RADIX], refs[RADIX]
    columns, nodes = features_ref.shape
    groups = nodes // LOW
    capacity = boundary_ref.shape[1]
    for high in range(groups):
        rows_ref[pl.ds(high * columns, columns), :] = features_ref[:, pl.ds(high * LOW, LOW)]
    slot = lax.broadcasted_iota(jnp.int32, (1, capacity), 1)
    for k in range(RADIX):
        for j in range(RADIX):
            p = relative(place_ref[0], j, k)
            listed = boundary_ref[pl.ds(p, 1), :]
            used = slot < counts_ref[0, p]
            high = jnp.where(used, listed >> 8, -1)
            low = (listed & (LOW - 1)).astype(jnp.float32)
            found = jnp.dot(rows_ref[...], one_hot(low, LOW), preferred_element_type=jnp.float32)
            total = jnp.zeros((columns, capacity), jnp.float32)
            for group in range(groups):
                total = total + jnp.where(high == group, found[group * columns:(group + 1) * columns], 0.0)
            out_refs[k][j] = total.astype(jnp.bfloat16)


def pick(place, features, boundary, counts):
    columns, nodes = features.shape
    capacity = boundary.shape[1]
    vm = pl.BlockSpec(memory_space=pltpu.VMEM)
    sm = pl.BlockSpec(memory_space=pltpu.SMEM)
    return pl.pallas_call(
        pick_kernel,
        out_shape=(jax.ShapeDtypeStruct((RADIX, columns, capacity), jnp.bfloat16),) * RADIX,
        in_specs=[sm, vm, vm, sm],
        out_specs=(vm,) * RADIX,
        scratch_shapes=[pltpu.VMEM((columns * nodes // LOW, LOW), jnp.bfloat16)],
        compiler_params=pltpu.CompilerParams(vmem_limit_bytes=VMEM),
        name="pick",
    )(place, features, boundary, counts)


def regroup_kernel(*refs):
    in_refs, out_refs = refs[:RADIX], refs[RADIX:]
    for j, out_ref in enumerate(out_refs, 1):
        for k, in_ref in enumerate(in_refs):
            out_ref[k] = in_ref[j]


def regroup(pieces):
    vm = pl.BlockSpec(memory_space=pltpu.VMEM)
    return pl.pallas_call(
        regroup_kernel,
        out_shape=(jax.ShapeDtypeStruct(pieces[0].shape, jnp.bfloat16),) * (RADIX - 1),
        in_specs=[vm] * RADIX,
        out_specs=(vm,) * (RADIX - 1),
        name="regroup",
    )(*pieces)


def pack_kernel(parity_ref, features_ref, neigh_weight_ref, self_weight_ref, cotangent_ref, bias_ref,
                inputs_ref, traded_ref):
    shares, _, width = inputs_ref.shape
    half = features_ref.shape[1] // 2
    wide = (width - half) // 2
    for share in range(shares):
        inputs_ref[share, :, pl.ds(0, half)] = features_ref[:, pl.ds((share % 2) * half, half)]
        at = pl.ds((share // 2) * wide, wide)
        inputs_ref[share, :, pl.ds(half, wide)] = neigh_weight_ref[:, at]
        inputs_ref[share, :, pl.ds(half + wide, wide)] = self_weight_ref[:, at]
    hidden = cotangent_ref.shape[0]
    traded_ref[pl.ds(0, hidden), :] = cotangent_ref[
        :, pl.ds(pl.multiple_of((1 - parity_ref[0]) * half, half), half)]
    bias = jnp.concatenate([bias_ref[...], jnp.zeros((1, half - hidden), jnp.bfloat16)], axis=1)
    traded_ref[pl.ds(hidden, EXTRA), :] = jnp.broadcast_to(bias.astype(jnp.float32), (EXTRA, half)).astype(jnp.bfloat16)


def pack(parity, features, neigh_weight, self_weight, cotangent, bias, shares):
    columns = features.shape[0]
    hidden, seed_count = cotangent.shape
    half = seed_count // 2
    whole = lambda i: (0, 0)
    return pl.pallas_call(
        pack_kernel,
        grid=(1,),
        out_shape=(jax.ShapeDtypeStruct((shares, columns, half + 4 * hidden), jnp.bfloat16),
                   jax.ShapeDtypeStruct((hidden + EXTRA, half), jnp.bfloat16)),
        in_specs=[pl.BlockSpec(memory_space=pltpu.SMEM),
                  pl.BlockSpec((columns, seed_count), whole),
                  pl.BlockSpec(neigh_weight.shape, whole),
                  pl.BlockSpec(self_weight.shape, whole),
                  pl.BlockSpec(cotangent.shape, whole),
                  pl.BlockSpec(bias.shape, whole)],
        out_specs=(pl.BlockSpec((shares, columns, half + 4 * hidden), lambda i: (0, 0, 0)),
                   pl.BlockSpec((hidden + EXTRA, half), whole)),
        compiler_params=pltpu.CompilerParams(vmem_limit_bytes=VMEM),
        name="pack",
    )(parity, features, neigh_weight, self_weight, cotangent, bias)


def fill_table(first_group, groups, rank_ref, low_ref, store):
    def pairs(i, carry):
        for unrolled in range(UNROLL):
            pair = i * UNROLL + unrolled
            found = []
            for k in range(2):
                group = first_group + 2 * pair + k
                rank = rank_ref[pl.ds(group, 1), :]
                named = jnp.where(rank < 0, 0.0, 1.0)
                left = one_hot_small(jnp.maximum(rank, 0.0), named, rank.shape[1])
                right = one_hot_small(low_ref[pl.ds(group, 1), :], named, LOW)
                table = lax.dot_general(left, right, NT, preferred_element_type=jnp.float32)
                found.append(table.reshape(table.shape[0] // GROUP, GROUP, LOW))
            rows = pl.ds(pl.multiple_of(pair * 2 * GROUP, 2 * GROUP), 2 * GROUP)
            store(rows, jnp.concatenate(found, axis=1).astype(jnp.bfloat16))
        return carry

    lax.fori_loop(0, groups // 2 // UNROLL, pairs, 0)


def table_kernel(neighbors_ref, features_ref, remote_ref, local_ref, rank_ref, low_ref, local_table_ref):
    slot_count, seed_count = neighbors_ref.shape
    group_count = seed_count // GROUP
    rows, half = local_table_ref.shape
    highs = half // LOW
    step = pl.program_id(0)

    @pl.when(step == 0)
    def _():
        values = []
        for member in range(GROUP):
            value = neighbors_ref[:, pl.ds(member * group_count, group_count)].astype(jnp.float32)
            values.append(jnp.concatenate(
                [value, jnp.full((PAD - slot_count, group_count), -1.0, jnp.float32)], axis=0))
        value = jnp.concatenate(values, axis=0).T
        member = lax.broadcasted_iota(jnp.int32, value.shape, 1) // PAD
        high = jnp.floor(value * (1.0 / LOW))
        rank_ref[...] = jnp.where(value < 0, -1.0, high * GROUP + member.astype(jnp.float32))
        low_ref[...] = value - high * LOW

    def store(at, table):
        for high in range(highs):
            local_table_ref[at, pl.ds(high * LOW, LOW)] = table[high]
            remote_ref[at, pl.ds(high * LOW, LOW)] = table[highs + high]

    groups = rows // GROUP
    fill_table(step * groups, groups, rank_ref, low_ref, store)
    local_ref[...] = lax.dot_general(
        local_table_ref[...], features_ref[...], NT, preferred_element_type=jnp.float32)


def first_tables(neighbors, features, blocks, rows=256):
    slot_count, seed_count = neighbors.shape
    columns, nodes = features.shape
    group_count = seed_count // GROUP
    keys = jax.ShapeDtypeStruct((group_count, GROUP * PAD), jnp.float32)
    whole = lambda i: (0, 0)
    return pl.pallas_call(
        table_kernel,
        grid=(blocks,),
        out_shape=(jax.ShapeDtypeStruct((blocks * rows, nodes), jnp.bfloat16),
                   jax.ShapeDtypeStruct((blocks * rows, columns), jnp.float32), keys, keys),
        in_specs=[pl.BlockSpec((slot_count, seed_count), whole), pl.BlockSpec((columns, nodes), whole)],
        out_specs=(pl.BlockSpec((rows, nodes), lambda i: (i, 0)),
                   pl.BlockSpec((rows, columns), lambda i: (i, 0)),
                   pl.BlockSpec(keys.shape, whole), pl.BlockSpec(keys.shape, whole)),
        scratch_shapes=[pltpu.VMEM((rows, nodes), jnp.bfloat16)],
        compiler_params=pltpu.CompilerParams(vmem_limit_bytes=VMEM),
        name="first_tables",
    )(neighbors, features)


def mean_kernel(rows, place_ref, remote_ref, near_refs, far_refs, local_ref, rank_ref, low_ref, neighbors_ref,
                features_ref, out_ref, lookup_ref, sum_ref, table_ref, held_ref, sems):
    _, columns, capacity = near_refs[0].shape
    nodes = features_ref.shape[1]
    seed_count = sum_ref.shape[0]
    group_count = seed_count // GROUP
    blocks = held_ref.shape[0]
    copies = [
        pltpu.make_async_copy(remote_ref.at[pl.ds(k * rows, rows), :], held_ref.at[k], sems.at[k])
        for k in range(blocks)]
    for copy in copies:
        copy.start()
    lookup_ref[:, pl.ds(0, nodes)] = features_ref[...]
    for j in range(RADIX):
        for k in range(RADIX):
            source = relative(place_ref[0], RADIX - j, RADIX - k)
            at = pl.ds(pl.multiple_of(nodes + source * capacity, capacity), capacity)
            lookup_ref[:, at] = near_refs[k][0] if j == 0 else far_refs[j - 1][k]

    def store(at, table):
        for high in range(table.shape[0]):
            table_ref[at, pl.ds(high * LOW, LOW)] = table[high]

    def build(k, carry):
        fill_table(k * (rows // GROUP), rows // GROUP, rank_ref, low_ref, store)
        sum_ref[pl.ds(pl.multiple_of(k * rows, rows), rows), pl.ds(0, columns)] = lax.dot_general(
            table_ref[...], lookup_ref[...], NT, preferred_element_type=jnp.float32)
        return carry

    lax.fori_loop(blocks, seed_count // rows, build, 0)
    for k in range(blocks):
        copies[k].wait()
        at = pl.ds(k * rows, rows)
        sum_ref[at, pl.ds(0, columns)] = local_ref[at, :] + lax.dot_general(
            held_ref[k], lookup_ref[:, nodes:], NT, preferred_element_type=jnp.float32)

    degree = jnp.sum(jnp.where(neighbors_ref[...] >= 0, 1.0, 0.0), axis=0, keepdims=True)
    shares, _, half = out_ref.shape
    for member in range(GROUP):
        mine = sum_ref[pl.ds(member, group_count, stride=GROUP), :].T[:columns]
        start = member * group_count
        mine = mine / degree[:, start:start + group_count]
        mine = mine.astype(jnp.bfloat16)
        for share in range(start // half, shares, 2):
            out_ref[share, :, pl.ds(start % half, group_count)] = mine


def neighbor_mean(place, remote, near, far, local, rank, low, neighbors, features, shares, rows=256):
    slot_count, seed_count = neighbors.shape
    columns, nodes = features.shape
    capacity = near[0].shape[2]
    blocks = remote.shape[0] // rows
    lookup_width = nodes + RADIX * RADIX * capacity
    vm = pl.BlockSpec(memory_space=pltpu.VMEM)

    def kernel(place_ref, remote_ref, *refs):
        mean_kernel(rows, place_ref, remote_ref, refs[:RADIX], refs[RADIX:2 * RADIX - 1], *refs[2 * RADIX - 1:])

    return pl.pallas_call(
        kernel,
        out_shape=jax.ShapeDtypeStruct((shares, columns, seed_count // 2), jnp.bfloat16),
        in_specs=[pl.BlockSpec(memory_space=pltpu.SMEM), pl.BlockSpec(memory_space=pl.ANY)]
        + [vm] * (2 * RADIX - 1 + 5),
        out_specs=vm,
        scratch_shapes=[pltpu.VMEM((columns, lookup_width), jnp.bfloat16),
                        pltpu.VMEM((seed_count, 128), jnp.float32),
                        pltpu.VMEM((rows, lookup_width), jnp.bfloat16),
                        pltpu.VMEM((blocks, rows, nodes), jnp.bfloat16),
                        pltpu.SemaphoreType.DMA((blocks,))],
        compiler_params=pltpu.CompilerParams(vmem_limit_bytes=VMEM),
        name="mean",
    )(place, remote, *near, *far, local, rank, low, neighbors, features)


def layer_kernel(parity_ref, own_ref, mean_ref, neigh_weight_ref, self_weight_ref, bias_ref, cotangent_ref,
                 traded_ref, traded_bias_ref, kept_ref, sent_ref, grad_ref, total_ref, sums_ref):
    step = pl.program_id(0)
    odd = parity_ref[0] == 1
    hidden = cotangent_ref.shape[0]

    @pl.when(step == 0)
    def _():
        total_ref[...] = jnp.zeros_like(total_ref)
        sums_ref[...] = jnp.zeros_like(sums_ref)

    def ordered(mine, other):
        return jnp.concatenate([jnp.where(odd, other, mine), jnp.where(odd, mine, other)], axis=0)

    mine = bias_ref[...].astype(jnp.float32)
    theirs = traded_bias_ref[:1, :hidden].astype(jnp.float32)
    bias = jnp.concatenate([jnp.where(odd, theirs, mine), jnp.where(odd, mine, theirs)], axis=1)
    row = lax.broadcasted_iota(jnp.int32, (EXTRA, 2 * hidden), 0)
    bias = jnp.where(row == 0, bias, 0.0).astype(jnp.bfloat16)
    ones = jnp.ones((EXTRA, own_ref.shape[1]), jnp.bfloat16)
    cotangent = ordered(cotangent_ref[...].astype(jnp.float32), traded_ref[...].astype(jnp.float32))
    preact = (
        lax.dot_general(neigh_weight_ref[...], mean_ref[...], TN, preferred_element_type=jnp.float32)
        + lax.dot_general(self_weight_ref[...], own_ref[...], TN, preferred_element_type=jnp.float32)
        + lax.dot_general(bias, ones, TN, preferred_element_type=jnp.float32)
    )
    decay = jnp.exp(jnp.minimum(preact, 0.0))
    activation = jnp.where(preact > 0, preact, decay - 1.0)
    kept_ref[...] = jnp.where(odd, activation[hidden:], activation[:hidden]).astype(jnp.bfloat16)
    sent_ref[...] = jnp.where(odd, activation[:hidden], activation[hidden:]).astype(jnp.bfloat16)
    slope = jnp.where(preact > 0, 1.0, decay)
    grad_pre = (cotangent * slope).astype(jnp.bfloat16)
    first, second = grad_pre[:hidden], grad_pre[hidden:]
    blank = jnp.zeros_like(first)
    for_neigh = jnp.concatenate([first, blank, second, blank], axis=0)
    for_own = jnp.concatenate([blank, first, blank, second], axis=0)
    total_ref[...] += (
        lax.dot_general(mean_ref[...], for_neigh, NT, preferred_element_type=jnp.float32)
        + lax.dot_general(own_ref[...], for_own, NT, preferred_element_type=jnp.float32))
    sums_ref[...] += lax.dot_general(ones[:SUMS], for_neigh, NT, preferred_element_type=jnp.float32)

    @pl.when(step == pl.num_programs(0) - 1)
    def _():
        chunks, rows, width = grad_ref.shape
        columns = rows - SUMS
        sums = sums_ref[...]
        high = sums.astype(jnp.bfloat16).astype(jnp.float32)
        row = lax.broadcasted_iota(jnp.int32, sums.shape, 0)
        extra = jnp.where(row == 0, high, jnp.where(row == 1, sums - high, 0.0))
        for chunk in range(chunks):
            at = slice((chunk % 2) * width, (chunk % 2 + 1) * width)
            mine = total_ref[pl.ds((chunk // 2) * columns, columns), at]
            grad_ref[chunk] = jnp.concatenate([mine, extra[:, at]], axis=0).astype(jnp.bfloat16)


def layer(parity, inputs, mean, bias, cotangent, traded, shares, block=512):
    features, half = mean.shape
    hidden = cotangent.shape[0]
    pair = 2 * hidden
    blocks = half // block
    whole = lambda i, parity: (0, 0)
    part = lambda i, parity: (0, i)
    grads = (2 * shares, features // shares + SUMS, pair)
    return pl.pallas_call(
        layer_kernel,
        grid_spec=pltpu.PrefetchScalarGridSpec(
            num_scalar_prefetch=1,
            grid=(blocks,),
            in_specs=[pl.BlockSpec((features, block), part),
                      pl.BlockSpec((features, block), part),
                      pl.BlockSpec((features, pair), lambda i, parity: (0, half // pair)),
                      pl.BlockSpec((features, pair), lambda i, parity: (0, half // pair + 1)),
                      pl.BlockSpec((1, hidden), whole),
                      pl.BlockSpec((hidden, block), lambda i, parity: (0, i + parity[0] * blocks)),
                      pl.BlockSpec((hidden, block), part),
                      pl.BlockSpec((EXTRA, 128), lambda i, parity: (hidden // EXTRA, 0))],
            out_specs=(pl.BlockSpec((hidden, block), part),
                       pl.BlockSpec((hidden, block), part),
                       pl.BlockSpec(grads, lambda i, parity: (0, 0, 0))),
            scratch_shapes=[pltpu.VMEM((features, 2 * pair), jnp.float32),
                            pltpu.VMEM((SUMS, 2 * pair), jnp.float32)]),
        out_shape=(jax.ShapeDtypeStruct((hidden, half), jnp.bfloat16),
                   jax.ShapeDtypeStruct((hidden, half), jnp.bfloat16),
                   jax.ShapeDtypeStruct(grads, jnp.bfloat16)),
        compiler_params=pltpu.CompilerParams(vmem_limit_bytes=VMEM // 2),
        name="layer",
    )(parity, inputs, mean, inputs, inputs, bias, cotangent, traded, traded)


def gradient_holders(shares, partitions):
    side, depth = math.isqrt(shares), partitions // 2
    ring = lambda a, b, size: min((a - b) % size, (b - a) % size)
    holders = []
    for f in range(shares):
        flat = lambda g: ring(g // side, f // side, side) + ring(g % side, f % side, side)
        rise = lambda v: 2 * ring(v // 2, f // 2, depth) + (v % 2 != f % 2)
        row = [0] * shares
        for v, g in zip(sorted(range(partitions), key=rise), sorted(range(shares), key=flat, reverse=True)):
            row[g] = v
        holders.append(row)
    return holders


def body(features, neigh_weight, self_weight, bias, neighbors, boundary, counts, cotangent):
    columns, nodes = features.shape
    partitions = lax.axis_size("vertex")
    shares = lax.axis_size("feat")
    seed_count = neighbors.shape[1]
    hidden = cotangent.shape[0]
    pair = 2 * hidden
    odd = lax.axis_index("feat") % 2
    parity = odd.astype(jnp.int32).reshape(1)
    bias = bias.reshape(1, hidden)
    trade = [(f, f ^ 1) for f in range(shares)]

    place = lax.axis_index("vertex").astype(jnp.int32).reshape(1)
    near = list(pick(place, features, boundary[0], counts))
    near[1:], late = lax.optimization_barrier((near[1:], parity))
    for k in range(1, RADIX):
        near[k] = lax.ppermute(
            near[k], "vertex", [(v, v // RADIX * RADIX + (v + k) % RADIX) for v in range(partitions)])
    inputs, traded = pack(late, features, neigh_weight, self_weight, cotangent, bias, shares)
    near[1:], inputs = lax.optimization_barrier((near[1:], inputs))
    far = list(regroup(near))
    far, early, traded, inputs = lax.optimization_barrier((far, neighbors, traded, inputs))
    inputs = lax.all_to_all(inputs, "feat", split_axis=0, concat_axis=0, tiled=True)
    for j in range(1, RADIX):
        far[j - 1] = lax.ppermute(
            far[j - 1], "vertex", [(v, (v + j * RADIX) % partitions) for v in range(partitions)])
    traded = lax.ppermute(traded, "feat", trade)
    remote, local, rank, low = first_tables(early, features, FIRST)
    mean = neighbor_mean(place, remote, near, far, local, rank, low, neighbors, features, shares)
    mean, inputs, traded, parity = lax.optimization_barrier((mean, inputs, traded, parity))
    inputs = inputs.reshape(shares * columns, inputs.shape[2])
    mean = lax.all_to_all(mean, "feat", split_axis=0, concat_axis=0, tiled=True)
    mean = mean.reshape(shares * columns, mean.shape[2])
    kept, sent, grad = layer(parity, inputs, mean, bias, cotangent, traded, shares)
    holders = gradient_holders(shares, partitions)
    members = [[holders[2 * q + k][g] * shares + 2 * q + k for g in range(shares) for k in range(2)]
               for q in range(shares // 2)]
    grad = lax.all_to_all(
        grad, ("vertex", "feat"), split_axis=0, concat_axis=0, tiled=True, axis_index_groups=members)
    other = lax.ppermute(sent, "feat", trade)
    activation = jnp.concatenate(
        [jnp.where(odd == 1, other, kept), jnp.where(odd == 1, kept, other)], axis=1)

    factor = 1.0 / math.sqrt(seed_count * partitions)
    grad = jnp.sum(grad.astype(jnp.float32), axis=0) * factor
    bias_out = grad[columns, :hidden] + grad[columns + 1, :hidden]
    swap = [(holders[f][g] * shares + f, f * shares + g) for f in range(shares) for g in range(shares)]
    grad = lax.ppermute(grad[:columns], ("vertex", "feat"), swap)
    return activation, grad[:, :hidden], grad[:, hidden:], bias_out


def solution(mesh):
    placed = (
        P("feat", "vertex"),
        P("feat", None),
        P("feat", None),
        P("feat"),
        P(None, "vertex"),
        P("vertex", None, None),
        P("vertex", None),
        P("feat", "vertex"),
    )
    return jax.shard_map(
        body,
        mesh=mesh,
        in_specs=placed,
        out_specs=(P("feat", "vertex"), P("feat", "vertex"), P("feat", "vertex"), P("feat")),
        check_vma=False,
    )
```

```python
import functools
import math

import jax
import jax.numpy as jnp
from jax import lax
from jax.experimental import pallas as pl
from jax.experimental.pallas import tpu as pltpu
from jax.sharding import PartitionSpec as P

LOW = 256
ONES = jnp.float8_e4m3fn
UNROLL = 16
FIRST = 5
RADIX = 4
PAD = 32
GROUP = 8
SUMS = 8
EXTRA = 16
VMEM = 60 * 1024 * 1024
NT = (((1,), (1,)), ((), ()))
TN = (((0,), (0,)), ((), ()))


def one_hot(keys, rows):
    width = keys.shape[1]
    wide = jnp.broadcast_to(keys, (16, width)).astype(jnp.bfloat16)
    base = lax.broadcasted_iota(jnp.int32, (rows, width), 0).astype(jnp.float32).astype(jnp.bfloat16)
    base = base.reshape(rows // 16, 16, width)
    hit = base == wide[None]
    return jnp.where(hit, jnp.bfloat16(1), jnp.bfloat16(0)).reshape(rows, width)


def relative(place, j, k):
    return ((place // RADIX + j) % RADIX) * RADIX + (place % RADIX + k) % RADIX


def one_hot_small(keys, ones, rows):
    width = keys.shape[1]
    wide = jnp.broadcast_to(keys - 128.0, (32, width)).astype(jnp.int32).astype(jnp.int8)
    ones = jnp.broadcast_to(ones, (32, width)).astype(ONES)
    base = (lax.broadcasted_iota(jnp.int32, (rows, width), 0) - 128).astype(jnp.int8)
    hit = base.reshape(rows // 32, 32, width) == wide[None]
    return jnp.where(hit, ones[None], jnp.zeros((), ONES)).reshape(rows, width)


def pick_kernel(place_ref, features_ref, boundary_ref, counts_ref, *refs):
    out_refs, rows_ref = refs[:RADIX], refs[RADIX]
    columns, nodes = features_ref.shape
    groups = nodes // LOW
    capacity = boundary_ref.shape[1]
    for high in range(groups):
        rows_ref[pl.ds(high * columns, columns), :] = features_ref[:, pl.ds(high * LOW, LOW)]
    slot = lax.broadcasted_iota(jnp.int32, (1, capacity), 1)
    for k in range(RADIX):
        for j in range(RADIX):
            p = relative(place_ref[0], j, k)
            listed = boundary_ref[pl.ds(p, 1), :]
            used = slot < counts_ref[0, p]
            high = jnp.where(used, listed >> 8, -1)
            low = (listed & (LOW - 1)).astype(jnp.float32)
            found = jnp.dot(rows_ref[...], one_hot(low, LOW), preferred_element_type=jnp.float32)
            total = jnp.zeros((columns, capacity), jnp.float32)
            for group in range(groups):
                total = jnp.where(high == group, found[group * columns:(group + 1) * columns], total)
            out_refs[k][j] = total.astype(jnp.bfloat16)


def pick(place, features, boundary, counts):
    columns, nodes = features.shape
    capacity = boundary.shape[1]
    vm = pl.BlockSpec(memory_space=pltpu.VMEM)
    sm = pl.BlockSpec(memory_space=pltpu.SMEM)
    return pl.pallas_call(
        pick_kernel,
        out_shape=(jax.ShapeDtypeStruct((RADIX, columns, capacity), jnp.bfloat16),) * RADIX,
        in_specs=[sm, vm, vm, sm],
        out_specs=(vm,) * RADIX,
        scratch_shapes=[pltpu.VMEM((columns * nodes // LOW, LOW), jnp.bfloat16)],
        compiler_params=pltpu.CompilerParams(vmem_limit_bytes=VMEM),
        name="pick",
    )(place, features, boundary, counts)


def regroup_kernel(*refs):
    in_refs, out_refs = refs[:RADIX], refs[RADIX:]
    for j, out_ref in enumerate(out_refs, 1):
        for k, in_ref in enumerate(in_refs):
            out_ref[k] = in_ref[j]


def regroup(pieces):
    vm = pl.BlockSpec(memory_space=pltpu.VMEM)
    return pl.pallas_call(
        regroup_kernel,
        out_shape=(jax.ShapeDtypeStruct(pieces[0].shape, jnp.bfloat16),) * (RADIX - 1),
        in_specs=[vm] * RADIX,
        out_specs=(vm,) * (RADIX - 1),
        name="regroup",
    )(*pieces)


def pack_kernel(parity_ref, features_ref, neigh_weight_ref, self_weight_ref, cotangent_ref, bias_ref,
                inputs_ref, traded_ref):
    shares, _, width = inputs_ref.shape
    half = features_ref.shape[1] // 2
    wide = (width - half) // 2
    for share in range(shares):
        inputs_ref[share, :, pl.ds(0, half)] = features_ref[:, pl.ds((share % 2) * half, half)]
        at = pl.ds((share // 2) * wide, wide)
        inputs_ref[share, :, pl.ds(half, wide)] = neigh_weight_ref[:, at]
        inputs_ref[share, :, pl.ds(half + wide, wide)] = self_weight_ref[:, at]
    hidden = cotangent_ref.shape[0]
    traded_ref[pl.ds(0, hidden), :] = cotangent_ref[
        :, pl.ds(pl.multiple_of((1 - parity_ref[0]) * half, half), half)]
    bias = jnp.concatenate([bias_ref[...], jnp.zeros((1, half - hidden), jnp.bfloat16)], axis=1)
    traded_ref[pl.ds(hidden, EXTRA), :] = jnp.broadcast_to(bias.astype(jnp.float32), (EXTRA, half)).astype(jnp.bfloat16)


def pack(parity, features, neigh_weight, self_weight, cotangent, bias, shares):
    columns = features.shape[0]
    hidden, seed_count = cotangent.shape
    half = seed_count // 2
    whole = lambda i: (0, 0)
    return pl.pallas_call(
        pack_kernel,
        grid=(1,),
        out_shape=(jax.ShapeDtypeStruct((shares, columns, half + 4 * hidden), jnp.bfloat16),
                   jax.ShapeDtypeStruct((hidden + EXTRA, half), jnp.bfloat16)),
        in_specs=[pl.BlockSpec(memory_space=pltpu.SMEM),
                  pl.BlockSpec((columns, seed_count), whole),
                  pl.BlockSpec(neigh_weight.shape, whole),
                  pl.BlockSpec(self_weight.shape, whole),
                  pl.BlockSpec(cotangent.shape, whole),
                  pl.BlockSpec(bias.shape, whole)],
        out_specs=(pl.BlockSpec((shares, columns, half + 4 * hidden), lambda i: (0, 0, 0)),
                   pl.BlockSpec((hidden + EXTRA, half), whole)),
        compiler_params=pltpu.CompilerParams(vmem_limit_bytes=VMEM),
        name="pack",
    )(parity, features, neigh_weight, self_weight, cotangent, bias)


def fill_table(first_group, groups, rank_ref, low_ref, store):
    def pairs(i, carry):
        for unrolled in range(UNROLL):
            pair = i * UNROLL + unrolled
            found = []
            for k in range(2):
                group = first_group + 2 * pair + k
                rank = rank_ref[pl.ds(group, 1), :]
                named = jnp.where(rank < 0, 0.0, 1.0)
                left = one_hot_small(jnp.maximum(rank, 0.0), named, rank.shape[1])
                right = one_hot_small(low_ref[pl.ds(group, 1), :], named, LOW)
                table = lax.dot_general(left, right, NT, preferred_element_type=jnp.float32)
                found.append(table.reshape(table.shape[0] // GROUP, GROUP, LOW))
            rows = pl.ds(pl.multiple_of(pair * 2 * GROUP, 2 * GROUP), 2 * GROUP)
            store(rows, jnp.concatenate(found, axis=1).astype(jnp.bfloat16))
        return carry

    lax.fori_loop(0, groups // 2 // UNROLL, pairs, 0)


def table_kernel(neighbors_ref, features_ref, remote_ref, local_ref, rank_ref, low_ref, local_table_ref):
    slot_count, seed_count = neighbors_ref.shape
    group_count = seed_count // GROUP
    rows, half = local_table_ref.shape
    highs = half // LOW
    step = pl.program_id(0)

    @pl.when(step == 0)
    def _():
        values = []
        for member in range(GROUP):
            value = neighbors_ref[:, pl.ds(member * group_count, group_count)].astype(jnp.float32)
            values.append(jnp.concatenate(
                [value, jnp.full((PAD - slot_count, group_count), -1.0, jnp.float32)], axis=0))
        value = jnp.concatenate(values, axis=0).T
        member = lax.broadcasted_iota(jnp.int32, value.shape, 1) // PAD
        high = jnp.floor(value * (1.0 / LOW))
        rank_ref[...] = jnp.where(value < 0, -1.0, high * GROUP + member.astype(jnp.float32))
        low_ref[...] = value - high * LOW

    def store(at, table):
        for high in range(highs):
            local_table_ref[at, pl.ds(high * LOW, LOW)] = table[high]
            remote_ref[at, pl.ds(high * LOW, LOW)] = table[highs + high]

    groups = rows // GROUP
    fill_table(step * groups, groups, rank_ref, low_ref, store)
    local_ref[...] = lax.dot_general(
        local_table_ref[...], features_ref[...], NT, preferred_element_type=jnp.float32)


def first_tables(neighbors, features, blocks, rows=256):
    slot_count, seed_count = neighbors.shape
    columns, nodes = features.shape
    group_count = seed_count // GROUP
    keys = jax.ShapeDtypeStruct((group_count, GROUP * PAD), jnp.float32)
    whole = lambda i: (0, 0)
    return pl.pallas_call(
        table_kernel,
        grid=(blocks,),
        out_shape=(jax.ShapeDtypeStruct((blocks * rows, nodes), jnp.bfloat16),
                   jax.ShapeDtypeStruct((blocks * rows, columns), jnp.float32), keys, keys),
        in_specs=[pl.BlockSpec((slot_count, seed_count), whole), pl.BlockSpec((columns, nodes), whole)],
        out_specs=(pl.BlockSpec((rows, nodes), lambda i: (i, 0)),
                   pl.BlockSpec((rows, columns), lambda i: (i, 0)),
                   pl.BlockSpec(keys.shape, whole), pl.BlockSpec(keys.shape, whole)),
        scratch_shapes=[pltpu.VMEM((rows, nodes), jnp.bfloat16)],
        compiler_params=pltpu.CompilerParams(vmem_limit_bytes=VMEM),
        name="first_tables",
    )(neighbors, features)


def mean_kernel(rows, place_ref, remote_ref, near_refs, far_refs, local_ref, rank_ref, low_ref, neighbors_ref,
                features_ref, out_ref, lookup_ref, sum_ref, table_ref, held_ref, sems):
    _, columns, capacity = near_refs[0].shape
    nodes = features_ref.shape[1]
    seed_count = sum_ref.shape[0]
    group_count = seed_count // GROUP
    blocks = held_ref.shape[0]
    copies = [
        pltpu.make_async_copy(remote_ref.at[pl.ds(k * rows, rows), :], held_ref.at[k], sems.at[k])
        for k in range(blocks)]
    for copy in copies:
        copy.start()
    lookup_ref[:, pl.ds(0, nodes)] = features_ref[...]
    for j in range(RADIX):
        for k in range(RADIX):
            source = relative(place_ref[0], RADIX - j, RADIX - k)
            at = pl.ds(pl.multiple_of(nodes + source * capacity, capacity), capacity)
            lookup_ref[:, at] = near_refs[k][0] if j == 0 else far_refs[j - 1][k]

    def store(at, table):
        for high in range(table.shape[0]):
            table_ref[at, pl.ds(high * LOW, LOW)] = table[high]

    def build(k, carry):
        fill_table(k * (rows // GROUP), rows // GROUP, rank_ref, low_ref, store)
        sum_ref[pl.ds(pl.multiple_of(k * rows, rows), rows), pl.ds(0, columns)] = lax.dot_general(
            table_ref[...], lookup_ref[...], NT, preferred_element_type=jnp.float32)
        return carry

    lax.fori_loop(blocks, seed_count // rows, build, 0)
    for k in range(blocks):
        copies[k].wait()
        at = pl.ds(k * rows, rows)
        sum_ref[at, pl.ds(0, columns)] = local_ref[at, :] + lax.dot_general(
            held_ref[k], lookup_ref[:, nodes:], NT, preferred_element_type=jnp.float32)

    degree = jnp.sum(jnp.where(neighbors_ref[...] >= 0, 1.0, 0.0), axis=0, keepdims=True)
    shares, _, half = out_ref.shape
    for member in range(GROUP):
        mine = sum_ref[pl.ds(member, group_count, stride=GROUP), :].T[:columns]
        start = member * group_count
        mine = mine / degree[:, start:start + group_count]
        mine = mine.astype(jnp.bfloat16)
        for share in range(start // half, shares, 2):
            out_ref[share, :, pl.ds(start % half, group_count)] = mine


def neighbor_mean(place, remote, near, far, local, rank, low, neighbors, features, shares, rows=256):
    slot_count, seed_count = neighbors.shape
    columns, nodes = features.shape
    capacity = near[0].shape[2]
    blocks = remote.shape[0] // rows
    lookup_width = nodes + RADIX * RADIX * capacity
    vm = pl.BlockSpec(memory_space=pltpu.VMEM)

    def kernel(place_ref, remote_ref, *refs):
        mean_kernel(rows, place_ref, remote_ref, refs[:RADIX], refs[RADIX:2 * RADIX - 1], *refs[2 * RADIX - 1:])

    return pl.pallas_call(
        kernel,
        out_shape=jax.ShapeDtypeStruct((shares, columns, seed_count // 2), jnp.bfloat16),
        in_specs=[pl.BlockSpec(memory_space=pltpu.SMEM), pl.BlockSpec(memory_space=pl.ANY)]
        + [vm] * (2 * RADIX - 1 + 5),
        out_specs=vm,
        scratch_shapes=[pltpu.VMEM((columns, lookup_width), jnp.bfloat16),
                        pltpu.VMEM((seed_count, 128), jnp.float32),
                        pltpu.VMEM((rows, lookup_width), jnp.bfloat16),
                        pltpu.VMEM((blocks, rows, nodes), jnp.bfloat16),
                        pltpu.SemaphoreType.DMA((blocks,))],
        compiler_params=pltpu.CompilerParams(vmem_limit_bytes=VMEM),
        name="mean",
    )(place, remote, *near, *far, local, rank, low, neighbors, features)


def layer_kernel(parity_ref, own_ref, mean_ref, neigh_weight_ref, self_weight_ref, bias_ref, cotangent_ref,
                 traded_ref, traded_bias_ref, kept_ref, sent_ref, grad_ref):
    odd = parity_ref[0] == 1
    hidden = cotangent_ref.shape[0]

    def ordered(mine, other):
        return jnp.concatenate([jnp.where(odd, other, mine), jnp.where(odd, mine, other)], axis=0)

    mine = bias_ref[...].astype(jnp.float32)
    theirs = traded_bias_ref[:1, :hidden].astype(jnp.float32)
    bias = jnp.concatenate([jnp.where(odd, theirs, mine), jnp.where(odd, mine, theirs)], axis=1)
    row = lax.broadcasted_iota(jnp.int32, (EXTRA, 2 * hidden), 0)
    bias = jnp.where(row == 0, bias, 0.0).astype(jnp.bfloat16)
    ones = jnp.ones((EXTRA, own_ref.shape[1]), jnp.bfloat16)
    cotangent = ordered(cotangent_ref[...].astype(jnp.float32), traded_ref[...].astype(jnp.float32))
    preact = (
        lax.dot_general(neigh_weight_ref[...], mean_ref[...], TN, preferred_element_type=jnp.float32)
        + lax.dot_general(self_weight_ref[...], own_ref[...], TN, preferred_element_type=jnp.float32)
        + lax.dot_general(bias, ones, TN, preferred_element_type=jnp.float32)
    )
    decay = jnp.exp(jnp.minimum(preact, 0.0))
    activation = jnp.where(preact > 0, preact, decay - 1.0)
    kept_ref[...] = jnp.where(odd, activation[hidden:], activation[:hidden]).astype(jnp.bfloat16)
    sent_ref[...] = jnp.where(odd, activation[:hidden], activation[hidden:]).astype(jnp.bfloat16)
    slope = jnp.where(preact > 0, 1.0, decay)
    grad_pre = (cotangent * slope).astype(jnp.bfloat16)
    first, second = grad_pre[:hidden], grad_pre[hidden:]
    blank = jnp.zeros_like(first)
    for_neigh = jnp.concatenate([first, blank, second, blank], axis=0)
    for_own = jnp.concatenate([blank, first, blank, second], axis=0)
    total = (
        lax.dot_general(mean_ref[...], for_neigh, NT, preferred_element_type=jnp.float32)
        + lax.dot_general(own_ref[...], for_own, NT, preferred_element_type=jnp.float32))
    sums = lax.dot_general(ones[:SUMS], for_neigh, NT, preferred_element_type=jnp.float32)
    chunks, rows, width = grad_ref.shape
    columns = rows - SUMS
    high = sums.astype(jnp.bfloat16).astype(jnp.float32)
    row = lax.broadcasted_iota(jnp.int32, sums.shape, 0)
    extra = jnp.where(row == 0, high, jnp.where(row == 1, sums - high, 0.0))
    for chunk in range(chunks):
        at = slice((chunk % 2) * width, (chunk % 2 + 1) * width)
        mine = total[(chunk // 2) * columns:(chunk // 2 + 1) * columns, at]
        grad_ref[chunk] = jnp.concatenate([mine, extra[:, at]], axis=0).astype(jnp.bfloat16)


def layer(parity, inputs, mean, bias, cotangent, traded, shares):
    features, half = mean.shape
    hidden = cotangent.shape[0]
    pair = 2 * hidden
    whole = lambda i, parity: (0, 0)
    grads = (2 * shares, features // shares + SUMS, pair)
    return pl.pallas_call(
        layer_kernel,
        grid_spec=pltpu.PrefetchScalarGridSpec(
            num_scalar_prefetch=1,
            grid=(1,),
            in_specs=[pl.BlockSpec((features, half), whole),
                      pl.BlockSpec((features, half), whole),
                      pl.BlockSpec((features, pair), lambda i, parity: (0, half // pair)),
                      pl.BlockSpec((features, pair), lambda i, parity: (0, half // pair + 1)),
                      pl.BlockSpec((1, hidden), whole),
                      pl.BlockSpec((hidden, half), lambda i, parity: (0, parity[0])),
                      pl.BlockSpec((hidden, half), whole),
                      pl.BlockSpec((EXTRA, 128), lambda i, parity: (hidden // EXTRA, 0))],
            out_specs=(pl.BlockSpec((hidden, half), whole),
                       pl.BlockSpec((hidden, half), whole),
                       pl.BlockSpec(grads, lambda i, parity: (0, 0, 0)))),
        out_shape=(jax.ShapeDtypeStruct((hidden, half), jnp.bfloat16),
                   jax.ShapeDtypeStruct((hidden, half), jnp.bfloat16),
                   jax.ShapeDtypeStruct(grads, jnp.bfloat16)),
        compiler_params=pltpu.CompilerParams(vmem_limit_bytes=VMEM // 2),
        name="layer",
    )(parity, inputs, mean, inputs, inputs, bias, cotangent, traded, traded)


def gradient_holders(shares, partitions):
    side, depth = math.isqrt(shares), partitions // 2
    ring = lambda a, b, size: min((a - b) % size, (b - a) % size)
    holders = []
    for f in range(shares):
        flat = lambda g: ring(g // side, f // side, side) + ring(g % side, f % side, side)
        rise = lambda v: 2 * ring(v // 2, f // 2, depth) + (v % 2 != f % 2)
        row = [0] * shares
        for v, g in zip(sorted(range(partitions), key=rise), sorted(range(shares), key=flat, reverse=True)):
            row[g] = v
        holders.append(row)
    return holders


def body(features, neigh_weight, self_weight, bias, neighbors, boundary, counts, cotangent):
    columns, nodes = features.shape
    partitions = lax.axis_size("vertex")
    shares = lax.axis_size("feat")
    seed_count = neighbors.shape[1]
    hidden = cotangent.shape[0]
    pair = 2 * hidden
    odd = lax.axis_index("feat") % 2
    parity = odd.astype(jnp.int32).reshape(1)
    bias = bias.reshape(1, hidden)
    trade = [(f, f ^ 1) for f in range(shares)]

    place = lax.axis_index("vertex").astype(jnp.int32).reshape(1)
    near = list(pick(place, features, boundary[0], counts))
    near[1:], late = lax.optimization_barrier((near[1:], parity))
    for k in range(1, RADIX):
        near[k] = lax.ppermute(
            near[k], "vertex", [(v, v // RADIX * RADIX + (v + k) % RADIX) for v in range(partitions)])
    inputs, traded = pack(late, features, neigh_weight, self_weight, cotangent, bias, shares)
    near[1:], inputs = lax.optimization_barrier((near[1:], inputs))
    far = list(regroup(near))
    far, early, traded, inputs = lax.optimization_barrier((far, neighbors, traded, inputs))
    inputs = lax.all_to_all(inputs, "feat", split_axis=0, concat_axis=0, tiled=True)
    for j in range(1, RADIX):
        far[j - 1] = lax.ppermute(
            far[j - 1], "vertex", [(v, (v + j * RADIX) % partitions) for v in range(partitions)])
    traded = lax.ppermute(traded, "feat", trade)
    remote, local, rank, low = first_tables(early, features, FIRST)
    mean = neighbor_mean(place, remote, near, far, local, rank, low, neighbors, features, shares)
    mean, inputs, traded, parity = lax.optimization_barrier((mean, inputs, traded, parity))
    inputs = inputs.reshape(shares * columns, inputs.shape[2])
    mean = lax.all_to_all(mean, "feat", split_axis=0, concat_axis=0, tiled=True)
    mean = mean.reshape(shares * columns, mean.shape[2])
    kept, sent, grad = layer(parity, inputs, mean, bias, cotangent, traded, shares)
    holders = gradient_holders(shares, partitions)
    members = [[holders[2 * q + k][g] * shares + 2 * q + k for g in range(shares) for k in range(2)]
               for q in range(shares // 2)]
    grad = lax.all_to_all(
        grad, ("vertex", "feat"), split_axis=0, concat_axis=0, tiled=True, axis_index_groups=members)
    other = lax.ppermute(sent, "feat", trade)
    activation = jnp.concatenate(
        [jnp.where(odd == 1, other, kept), jnp.where(odd == 1, kept, other)], axis=1)

    factor = 1.0 / math.sqrt(seed_count * partitions)
    grad = jnp.sum(grad.astype(jnp.float32), axis=0) * factor
    bias_out = grad[columns, :hidden] + grad[columns + 1, :hidden]
    swap = [(holders[f][g] * shares + f, f * shares + g) for f in range(shares) for g in range(shares)]
    grad = lax.ppermute(grad[:columns], ("vertex", "feat"), swap)
    return activation, grad[:, :hidden], grad[:, hidden:], bias_out


def solution(mesh):
    placed = (
        P("feat", "vertex"),
        P("feat", None),
        P("feat", None),
        P("feat"),
        P(None, "vertex"),
        P("vertex", None, None),
        P("vertex", None),
        P("feat", "vertex"),
    )
    return jax.shard_map(
        body,
        mesh=mesh,
        in_specs=placed,
        out_specs=(P("feat", "vertex"), P("feat", "vertex"), P("feat", "vertex"), P("feat")),
        check_vma=False,
    )
```

```python
import functools
import math

import jax
import jax.numpy as jnp
from jax import lax
from jax.experimental import pallas as pl
from jax.experimental.pallas import tpu as pltpu
from jax.sharding import PartitionSpec as P

LOW = 256
ONES = jnp.float8_e4m3fn
UNROLL = 16
FIRST = 6
RADIX = 4
PAD = 32
GROUP = 8
SUMS = 8
EXTRA = 16
VMEM = 60 * 1024 * 1024
NT = (((1,), (1,)), ((), ()))
TN = (((0,), (0,)), ((), ()))


def one_hot(keys, rows):
    width = keys.shape[1]
    wide = jnp.broadcast_to(keys, (16, width)).astype(jnp.bfloat16)
    base = lax.broadcasted_iota(jnp.int32, (rows, width), 0).astype(jnp.float32).astype(jnp.bfloat16)
    base = base.reshape(rows // 16, 16, width)
    hit = base == wide[None]
    return jnp.where(hit, jnp.bfloat16(1), jnp.bfloat16(0)).reshape(rows, width)


def relative(place, j, k):
    return ((place // RADIX + j) % RADIX) * RADIX + (place % RADIX + k) % RADIX


def one_hot_small(keys, ones, rows):
    width = keys.shape[1]
    wide = jnp.broadcast_to(keys - 128.0, (32, width)).astype(jnp.int32).astype(jnp.int8)
    ones = jnp.broadcast_to(ones, (32, width)).astype(ONES)
    base = (lax.broadcasted_iota(jnp.int32, (rows, width), 0) - 128).astype(jnp.int8)
    hit = base.reshape(rows // 32, 32, width) == wide[None]
    return jnp.where(hit, ones[None], jnp.zeros((), ONES)).reshape(rows, width)


def pick_kernel(place_ref, features_ref, boundary_ref, counts_ref, *refs):
    out_refs, rows_ref = refs[:RADIX], refs[RADIX]
    columns, nodes = features_ref.shape
    groups = nodes // LOW
    capacity = boundary_ref.shape[1]
    for high in range(groups):
        rows_ref[pl.ds(high * columns, columns), :] = features_ref[:, pl.ds(high * LOW, LOW)]
    slot = lax.broadcasted_iota(jnp.int32, (1, capacity), 1)
    for k in range(RADIX):
        for j in range(RADIX):
            p = relative(place_ref[0], j, k)
            listed = boundary_ref[pl.ds(p, 1), :]
            used = slot < counts_ref[0, p]
            high = jnp.where(used, listed >> 8, -1)
            low = (listed & (LOW - 1)).astype(jnp.float32)
            found = jnp.dot(rows_ref[...], one_hot(low, LOW), preferred_element_type=jnp.float32)
            total = jnp.zeros((columns, capacity), jnp.float32)
            for group in range(groups):
                total = jnp.where(high == group, found[group * columns:(group + 1) * columns], total)
            out_refs[k][j] = total.astype(jnp.bfloat16)


def pick(place, features, boundary, counts):
    columns, nodes = features.shape
    capacity = boundary.shape[1]
    vm = pl.BlockSpec(memory_space=pltpu.VMEM)
    sm = pl.BlockSpec(memory_space=pltpu.SMEM)
    return pl.pallas_call(
        pick_kernel,
        out_shape=(jax.ShapeDtypeStruct((RADIX, columns, capacity), jnp.bfloat16),) * RADIX,
        in_specs=[sm, vm, vm, sm],
        out_specs=(vm,) * RADIX,
        scratch_shapes=[pltpu.VMEM((columns * nodes // LOW, LOW), jnp.bfloat16)],
        compiler_params=pltpu.CompilerParams(vmem_limit_bytes=VMEM),
        name="pick",
    )(place, features, boundary, counts)


def regroup_kernel(*refs):
    in_refs, out_refs = refs[:RADIX], refs[RADIX:]
    for j, out_ref in enumerate(out_refs, 1):
        for k, in_ref in enumerate(in_refs):
            out_ref[k] = in_ref[j]


def regroup(pieces):
    vm = pl.BlockSpec(memory_space=pltpu.VMEM)
    return pl.pallas_call(
        regroup_kernel,
        out_shape=(jax.ShapeDtypeStruct(pieces[0].shape, jnp.bfloat16),) * (RADIX - 1),
        in_specs=[vm] * RADIX,
        out_specs=(vm,) * (RADIX - 1),
        name="regroup",
    )(*pieces)


def pack_kernel(parity_ref, features_ref, neigh_weight_ref, self_weight_ref, cotangent_ref, bias_ref,
                inputs_ref, traded_ref):
    shares, _, width = inputs_ref.shape
    half = features_ref.shape[1] // 2
    wide = (width - half) // 2
    for share in range(shares):
        inputs_ref[share, :, pl.ds(0, half)] = features_ref[:, pl.ds((share % 2) * half, half)]
        at = pl.ds((share // 2) * wide, wide)
        inputs_ref[share, :, pl.ds(half, wide)] = neigh_weight_ref[:, at]
        inputs_ref[share, :, pl.ds(half + wide, wide)] = self_weight_ref[:, at]
    hidden = cotangent_ref.shape[0]
    traded_ref[pl.ds(0, hidden), :] = cotangent_ref[
        :, pl.ds(pl.multiple_of((1 - parity_ref[0]) * half, half), half)]
    bias = jnp.concatenate([bias_ref[...], jnp.zeros((1, half - hidden), jnp.bfloat16)], axis=1)
    traded_ref[pl.ds(hidden, EXTRA), :] = jnp.broadcast_to(bias.astype(jnp.float32), (EXTRA, half)).astype(jnp.bfloat16)


def pack(parity, features, neigh_weight, self_weight, cotangent, bias, shares):
    columns = features.shape[0]
    hidden, seed_count = cotangent.shape
    half = seed_count // 2
    whole = lambda i: (0, 0)
    return pl.pallas_call(
        pack_kernel,
        grid=(1,),
        out_shape=(jax.ShapeDtypeStruct((shares, columns, half + 4 * hidden), jnp.bfloat16),
                   jax.ShapeDtypeStruct((hidden + EXTRA, half), jnp.bfloat16)),
        in_specs=[pl.BlockSpec(memory_space=pltpu.SMEM),
                  pl.BlockSpec((columns, seed_count), whole),
                  pl.BlockSpec(neigh_weight.shape, whole),
                  pl.BlockSpec(self_weight.shape, whole),
                  pl.BlockSpec(cotangent.shape, whole),
                  pl.BlockSpec(bias.shape, whole)],
        out_specs=(pl.BlockSpec((shares, columns, half + 4 * hidden), lambda i: (0, 0, 0)),
                   pl.BlockSpec((hidden + EXTRA, half), whole)),
        compiler_params=pltpu.CompilerParams(vmem_limit_bytes=VMEM),
        name="pack",
    )(parity, features, neigh_weight, self_weight, cotangent, bias)


def fill_table(first_group, groups, rank_ref, low_ref, store):
    def pairs(i, carry):
        for unrolled in range(UNROLL):
            pair = i * UNROLL + unrolled
            found = []
            for k in range(2):
                group = first_group + 2 * pair + k
                rank = rank_ref[pl.ds(group, 1), :]
                named = jnp.where(rank < 0, 0.0, 1.0)
                left = one_hot_small(jnp.maximum(rank, 0.0), named, rank.shape[1])
                right = one_hot_small(low_ref[pl.ds(group, 1), :], named, LOW)
                table = lax.dot_general(left, right, NT, preferred_element_type=jnp.float32)
                found.append(table.reshape(table.shape[0] // GROUP, GROUP, LOW))
            rows = pl.ds(pl.multiple_of(pair * 2 * GROUP, 2 * GROUP), 2 * GROUP)
            store(rows, jnp.concatenate(found, axis=1).astype(jnp.bfloat16))
        return carry

    lax.fori_loop(0, groups // 2 // UNROLL, pairs, 0)


def table_kernel(neighbors_ref, features_ref, remote_ref, local_ref, rank_ref, low_ref, local_table_ref):
    slot_count, seed_count = neighbors_ref.shape
    group_count = seed_count // GROUP
    rows, half = local_table_ref.shape
    highs = half // LOW
    step = pl.program_id(0)

    @pl.when(step == 0)
    def _():
        values = []
        for member in range(GROUP):
            value = neighbors_ref[:, pl.ds(member * group_count, group_count)].astype(jnp.float32)
            values.append(jnp.concatenate(
                [value, jnp.full((PAD - slot_count, group_count), -1.0, jnp.float32)], axis=0))
        value = jnp.concatenate(values, axis=0).T
        member = lax.broadcasted_iota(jnp.int32, value.shape, 1) // PAD
        high = jnp.floor(value * (1.0 / LOW))
        rank_ref[...] = jnp.where(value < 0, -1.0, high * GROUP + member.astype(jnp.float32))
        low_ref[...] = value - high * LOW

    def store(at, table):
        for high in range(highs):
            local_table_ref[at, pl.ds(high * LOW, LOW)] = table[high]
            remote_ref[at, pl.ds(high * LOW, LOW)] = table[highs + high]

    groups = rows // GROUP
    fill_table(step * groups, groups, rank_ref, low_ref, store)
    local_ref[...] = lax.dot_general(
        local_table_ref[...], features_ref[...], NT, preferred_element_type=jnp.float32)


def first_tables(neighbors, features, blocks, rows=256):
    slot_count, seed_count = neighbors.shape
    columns, nodes = features.shape
    group_count = seed_count // GROUP
    keys = jax.ShapeDtypeStruct((group_count, GROUP * PAD), jnp.float32)
    whole = lambda i: (0, 0)
    return pl.pallas_call(
        table_kernel,
        grid=(blocks,),
        out_shape=(jax.ShapeDtypeStruct((blocks * rows, nodes), jnp.bfloat16),
                   jax.ShapeDtypeStruct((blocks * rows, columns), jnp.float32), keys, keys),
        in_specs=[pl.BlockSpec((slot_count, seed_count), whole), pl.BlockSpec((columns, nodes), whole)],
        out_specs=(pl.BlockSpec((rows, nodes), lambda i: (i, 0)),
                   pl.BlockSpec((rows, columns), lambda i: (i, 0)),
                   pl.BlockSpec(keys.shape, whole), pl.BlockSpec(keys.shape, whole)),
        scratch_shapes=[pltpu.VMEM((rows, nodes), jnp.bfloat16)],
        compiler_params=pltpu.CompilerParams(vmem_limit_bytes=VMEM),
        name="first_tables",
    )(neighbors, features)


def mean_kernel(rows, place_ref, remote_ref, near_refs, far_refs, local_ref, rank_ref, low_ref, neighbors_ref,
                features_ref, out_ref, lookup_ref, sum_ref, table_ref, held_ref, sems):
    _, columns, capacity = near_refs[0].shape
    nodes = features_ref.shape[1]
    seed_count = sum_ref.shape[0]
    group_count = seed_count // GROUP
    blocks = held_ref.shape[0]
    copies = [
        pltpu.make_async_copy(remote_ref.at[pl.ds(k * rows, rows), :], held_ref.at[k], sems.at[k])
        for k in range(blocks)]
    for copy in copies:
        copy.start()
    lookup_ref[:, pl.ds(0, nodes)] = features_ref[...]
    for j in range(RADIX):
        for k in range(RADIX):
            source = relative(place_ref[0], RADIX - j, RADIX - k)
            at = pl.ds(pl.multiple_of(nodes + source * capacity, capacity), capacity)
            lookup_ref[:, at] = near_refs[k][0] if j == 0 else far_refs[j - 1][k]

    def store(at, table):
        for high in range(table.shape[0]):
            table_ref[at, pl.ds(high * LOW, LOW)] = table[high]

    def build(k, carry):
        fill_table(k * (rows // GROUP), rows // GROUP, rank_ref, low_ref, store)
        sum_ref[pl.ds(pl.multiple_of(k * rows, rows), rows), pl.ds(0, columns)] = lax.dot_general(
            table_ref[...], lookup_ref[...], NT, preferred_element_type=jnp.float32)
        return carry

    lax.fori_loop(blocks, seed_count // rows, build, 0)
    for k in range(blocks):
        copies[k].wait()
        at = pl.ds(k * rows, rows)
        sum_ref[at, pl.ds(0, columns)] = local_ref[at, :] + lax.dot_general(
            held_ref[k], lookup_ref[:, nodes:], NT, preferred_element_type=jnp.float32)

    degree = jnp.sum(jnp.where(neighbors_ref[...] >= 0, 1.0, 0.0), axis=0, keepdims=True)
    shares, _, half = out_ref.shape
    for member in range(GROUP):
        mine = sum_ref[pl.ds(member, group_count, stride=GROUP), :].T[:columns]
        start = member * group_count
        mine = mine / degree[:, start:start + group_count]
        mine = mine.astype(jnp.bfloat16)
        for share in range(start // half, shares, 2):
            out_ref[share, :, pl.ds(start % half, group_count)] = mine


def neighbor_mean(place, remote, near, far, local, rank, low, neighbors, features, shares, rows=256):
    slot_count, seed_count = neighbors.shape
    columns, nodes = features.shape
    capacity = near[0].shape[2]
    blocks = remote.shape[0] // rows
    lookup_width = nodes + RADIX * RADIX * capacity
    vm = pl.BlockSpec(memory_space=pltpu.VMEM)

    def kernel(place_ref, remote_ref, *refs):
        mean_kernel(rows, place_ref, remote_ref, refs[:RADIX], refs[RADIX:2 * RADIX - 1], *refs[2 * RADIX - 1:])

    return pl.pallas_call(
        kernel,
        out_shape=jax.ShapeDtypeStruct((shares, columns, seed_count // 2), jnp.bfloat16),
        in_specs=[pl.BlockSpec(memory_space=pltpu.SMEM), pl.BlockSpec(memory_space=pl.ANY)]
        + [vm] * (2 * RADIX - 1 + 5),
        out_specs=vm,
        scratch_shapes=[pltpu.VMEM((columns, lookup_width), jnp.bfloat16),
                        pltpu.VMEM((seed_count, 128), jnp.float32),
                        pltpu.VMEM((rows, lookup_width), jnp.bfloat16),
                        pltpu.VMEM((blocks, rows, nodes), jnp.bfloat16),
                        pltpu.SemaphoreType.DMA((blocks,))],
        compiler_params=pltpu.CompilerParams(vmem_limit_bytes=VMEM),
        name="mean",
    )(place, remote, *near, *far, local, rank, low, neighbors, features)


def layer_kernel(parity_ref, own_ref, mean_ref, neigh_weight_ref, self_weight_ref, bias_ref, cotangent_ref,
                 traded_ref, traded_bias_ref, kept_ref, sent_ref, grad_ref):
    odd = parity_ref[0] == 1
    hidden = cotangent_ref.shape[0]

    def ordered(mine, other):
        return jnp.concatenate([jnp.where(odd, other, mine), jnp.where(odd, mine, other)], axis=0)

    mine = bias_ref[...].astype(jnp.float32)
    theirs = traded_bias_ref[:1, :hidden].astype(jnp.float32)
    bias = jnp.concatenate([jnp.where(odd, theirs, mine), jnp.where(odd, mine, theirs)], axis=1)
    row = lax.broadcasted_iota(jnp.int32, (EXTRA, 2 * hidden), 0)
    bias = jnp.where(row == 0, bias, 0.0).astype(jnp.bfloat16)
    ones = jnp.ones((EXTRA, own_ref.shape[1]), jnp.bfloat16)
    cotangent = ordered(cotangent_ref[...].astype(jnp.float32), traded_ref[...].astype(jnp.float32))
    preact = (
        lax.dot_general(neigh_weight_ref[...], mean_ref[...], TN, preferred_element_type=jnp.float32)
        + lax.dot_general(self_weight_ref[...], own_ref[...], TN, preferred_element_type=jnp.float32)
        + lax.dot_general(bias, ones, TN, preferred_element_type=jnp.float32)
    )
    decay = jnp.exp(jnp.minimum(preact, 0.0))
    activation = jnp.where(preact > 0, preact, decay - 1.0)
    kept_ref[...] = jnp.where(odd, activation[hidden:], activation[:hidden]).astype(jnp.bfloat16)
    sent_ref[...] = jnp.where(odd, activation[:hidden], activation[hidden:]).astype(jnp.bfloat16)
    slope = jnp.where(preact > 0, 1.0, decay)
    grad_pre = (cotangent * slope).astype(jnp.bfloat16)
    first, second = grad_pre[:hidden], grad_pre[hidden:]
    blank = jnp.zeros_like(first)
    for_neigh = jnp.concatenate([first, blank, second, blank], axis=0)
    for_own = jnp.concatenate([blank, first, blank, second], axis=0)
    total = (
        lax.dot_general(mean_ref[...], for_neigh, NT, preferred_element_type=jnp.float32)
        + lax.dot_general(own_ref[...], for_own, NT, preferred_element_type=jnp.float32))
    sums = lax.dot_general(ones[:SUMS], for_neigh, NT, preferred_element_type=jnp.float32)
    chunks, rows, width = grad_ref.shape
    columns = rows - SUMS
    high = sums.astype(jnp.bfloat16).astype(jnp.float32)
    row = lax.broadcasted_iota(jnp.int32, sums.shape, 0)
    extra = jnp.where(row == 0, high, jnp.where(row == 1, sums - high, 0.0))
    for chunk in range(chunks):
        at = slice((chunk % 2) * width, (chunk % 2 + 1) * width)
        mine = total[(chunk // 2) * columns:(chunk // 2 + 1) * columns, at]
        grad_ref[chunk] = jnp.concatenate([mine, extra[:, at]], axis=0).astype(jnp.bfloat16)


def layer(parity, inputs, mean, bias, cotangent, traded, shares):
    features, half = mean.shape
    hidden = cotangent.shape[0]
    pair = 2 * hidden
    whole = lambda i, parity: (0, 0)
    grads = (2 * shares, features // shares + SUMS, pair)
    return pl.pallas_call(
        layer_kernel,
        grid_spec=pltpu.PrefetchScalarGridSpec(
            num_scalar_prefetch=1,
            grid=(1,),
            in_specs=[pl.BlockSpec((features, half), whole),
                      pl.BlockSpec((features, half), whole),
                      pl.BlockSpec((features, pair), lambda i, parity: (0, half // pair)),
                      pl.BlockSpec((features, pair), lambda i, parity: (0, half // pair + 1)),
                      pl.BlockSpec((1, hidden), whole),
                      pl.BlockSpec((hidden, half), lambda i, parity: (0, parity[0])),
                      pl.BlockSpec((hidden, half), whole),
                      pl.BlockSpec((EXTRA, 128), lambda i, parity: (hidden // EXTRA, 0))],
            out_specs=(pl.BlockSpec((hidden, half), whole),
                       pl.BlockSpec((hidden, half), whole),
                       pl.BlockSpec(grads, lambda i, parity: (0, 0, 0)))),
        out_shape=(jax.ShapeDtypeStruct((hidden, half), jnp.bfloat16),
                   jax.ShapeDtypeStruct((hidden, half), jnp.bfloat16),
                   jax.ShapeDtypeStruct(grads, jnp.bfloat16)),
        compiler_params=pltpu.CompilerParams(vmem_limit_bytes=VMEM // 2),
        name="layer",
    )(parity, inputs, mean, inputs, inputs, bias, cotangent, traded, traded)


def gradient_holders(shares, partitions):
    side, depth = math.isqrt(shares), partitions // 2
    ring = lambda a, b, size: min((a - b) % size, (b - a) % size)
    holders = []
    for f in range(shares):
        flat = lambda g: ring(g // side, f // side, side) + ring(g % side, f % side, side)
        rise = lambda v: 2 * ring(v // 2, f // 2, depth) + (v % 2 != f % 2)
        row = [0] * shares
        for v, g in zip(sorted(range(partitions), key=rise), sorted(range(shares), key=flat, reverse=True)):
            row[g] = v
        holders.append(row)
    return holders


def body(features, neigh_weight, self_weight, bias, neighbors, boundary, counts, cotangent):
    columns, nodes = features.shape
    partitions = lax.axis_size("vertex")
    shares = lax.axis_size("feat")
    seed_count = neighbors.shape[1]
    hidden = cotangent.shape[0]
    pair = 2 * hidden
    odd = lax.axis_index("feat") % 2
    parity = odd.astype(jnp.int32).reshape(1)
    bias = bias.reshape(1, hidden)
    trade = [(f, f ^ 1) for f in range(shares)]

    place = lax.axis_index("vertex").astype(jnp.int32).reshape(1)
    near = list(pick(place, features, boundary[0], counts))
    near[1:], late = lax.optimization_barrier((near[1:], parity))
    for k in range(1, RADIX):
        near[k] = lax.ppermute(
            near[k], "vertex", [(v, v // RADIX * RADIX + (v + k) % RADIX) for v in range(partitions)])
    inputs, traded = pack(late, features, neigh_weight, self_weight, cotangent, bias, shares)
    near[1:], inputs = lax.optimization_barrier((near[1:], inputs))
    far = list(regroup(near))
    far, early, traded, inputs = lax.optimization_barrier((far, neighbors, traded, inputs))
    inputs = lax.all_to_all(inputs, "feat", split_axis=0, concat_axis=0, tiled=True)
    for j in (2, 1, 3):
        far[j - 1] = lax.ppermute(
            far[j - 1], "vertex", [(v, (v + j * RADIX) % partitions) for v in range(partitions)])
    traded = lax.ppermute(traded, "feat", trade)
    remote, local, rank, low = first_tables(early, features, FIRST)
    mean = neighbor_mean(place, remote, near, far, local, rank, low, neighbors, features, shares)
    mean, inputs, traded, parity = lax.optimization_barrier((mean, inputs, traded, parity))
    inputs = inputs.reshape(shares * columns, inputs.shape[2])
    mean = lax.all_to_all(mean, "feat", split_axis=0, concat_axis=0, tiled=True)
    mean = mean.reshape(shares * columns, mean.shape[2])
    kept, sent, grad = layer(parity, inputs, mean, bias, cotangent, traded, shares)
    holders = gradient_holders(shares, partitions)
    members = [[holders[2 * q + k][g] * shares + 2 * q + k for g in range(shares) for k in range(2)]
               for q in range(shares // 2)]
    grad = lax.all_to_all(
        grad, ("vertex", "feat"), split_axis=0, concat_axis=0, tiled=True, axis_index_groups=members)
    other = lax.ppermute(sent, "feat", trade)
    activation = jnp.concatenate(
        [jnp.where(odd == 1, other, kept), jnp.where(odd == 1, kept, other)], axis=1)

    factor = 1.0 / math.sqrt(seed_count * partitions)
    grad = jnp.sum(grad.astype(jnp.float32), axis=0) * factor
    bias_out = grad[columns, :hidden] + grad[columns + 1, :hidden]
    swap = [(holders[f][g] * shares + f, f * shares + g) for f in range(shares) for g in range(shares)]
    grad = lax.ppermute(grad[:columns], ("vertex", "feat"), swap)
    return activation, grad[:, :hidden], grad[:, hidden:], bias_out


def solution(mesh):
    placed = (
        P("feat", "vertex"),
        P("feat", None),
        P("feat", None),
        P("feat"),
        P(None, "vertex"),
        P("vertex", None, None),
        P("vertex", None),
        P("feat", "vertex"),
    )
    return jax.shard_map(
        body,
        mesh=mesh,
        in_specs=placed,
        out_specs=(P("feat", "vertex"), P("feat", "vertex"), P("feat", "vertex"), P("feat")),
        check_vma=False,
    )
```
